256 devices in a mesh: dp: 16 (over y_hi, x, core), seq: 16 (over y_lo, z).
Axes of the slice: x: 4, y: 4 (y_hi: 2, y_lo: 2; y = y_hi * 2 + y_lo), z: 8, core: 2. Of those that a mesh axis runs over, the one named last changes fastest.
Arguments:
- query: bfloat16 [16, 2048, 2048], P('dp', 'seq'), may hold values from -700 to 700
- key: bfloat16 [16, 2048, 2048], P('dp', 'seq'), may hold values from -700 to 700
- value: bfloat16 [16, 2048, 2048], P('dp', 'seq'), may hold values from -6 to 6
- q_gain: float32 [128], replicated, may hold values from 0.5 to 5
- k_gain: float32 [128], replicated, may hold values from 0.5 to 5
- noise: bfloat16 [16, 2048, 2048], P('dp', 'seq'), may hold values from -5 to 5
- mean_codes: int32 [16, 2048, 2048], P('dp', 'seq'), may hold values from 24 to 207, as said below
- scale_exps: int32 [16, 2048, 16], P('dp', 'seq'), may hold values from -2 to 1
- step_index: int32 [16], P('dp'), may hold values from 1 to 9
- rewards: float32 [16], replicated, may hold values from -4 to 4
- group_ids: int32 [16], replicated, may hold values from 0 to 3, as said below
Outputs:
- grad_query: bfloat16 [16, 2048, 2048], P('dp', 'seq')
- grad_key: bfloat16 [16, 2048, 2048], P('dp', 'seq')
- grad_value: bfloat16 [16, 2048, 2048], P('dp', 'seq')
- q_gain_grad: float32 [128], replicated
- k_gain_grad: float32 [128], replicated
The draws below stay inside these ranges and needn't reach their ends.
Inputs may be any that keep to these rules, and one draw needn't show every extreme that they name: `mean_codes`: every code has an exponent field (c // 8) % 16 of 3 to 9. `group_ids`: each id names exactly four clips.
All inputs are finite; a program needn't handle non-finite values.
Results may differ from the reference program's by a relative error of at most 0.015.
The reference program's roundings to bfloat16 on the way count: a program that leaves them out, or rounds other values in their place, can miss the bound.
Values may be sent and summed in bfloat16 or wider, within the bound.
A program may use at most 64 MiB of HBM per device.

```python
import math
import jax
import jax.numpy as jnp
from jax import lax

HEADS = 16
D_HEAD = 128
STEPS = 10
CLIPS = 16
SEQ_LEN = 2048
GROUPS = 4


def shared_rows(key):
    head_shape = (CLIPS, SEQ_LEN, HEADS, D_HEAD)
    shared_base = jnp.clip(jax.random.normal(key, head_shape, jnp.float32), -4.0, 4.0)
    col_scale = jnp.exp(jax.random.uniform(jax.random.fold_in(key, 77), (HEADS, D_HEAD), jnp.float32, 0.0, math.log(10.0)))
    return (shared_base, col_scale)


def draw_query(key, part):
    shared_base, col_scale = shared_rows(key)
    key = jax.random.fold_in(key, 1)
    own_draw = jnp.clip(jax.random.normal(key, shared_base.shape, jnp.float32), -4.0, 4.0)
    row_scale = jnp.exp(jax.random.uniform(jax.random.fold_in(key, 2), shared_base.shape[:3] + (1,), jnp.float32, 0.0, math.log(10.0)))
    field_out = own_draw
    return (field_out * col_scale * row_scale).reshape(CLIPS, SEQ_LEN, HEADS * D_HEAD).astype(jnp.bfloat16)


def draw_key(key, part):
    shared_base, col_scale = shared_rows(key)
    key = jax.random.fold_in(key, 3)
    own_draw = jnp.clip(jax.random.normal(key, shared_base.shape, jnp.float32), -4.0, 4.0)
    row_scale = jnp.exp(jax.random.uniform(jax.random.fold_in(key, 4), shared_base.shape[:3] + (1,), jnp.float32, 0.0, math.log(10.0)))
    field_out = own_draw
    return (field_out * col_scale * row_scale).reshape(CLIPS, SEQ_LEN, HEADS * D_HEAD).astype(jnp.bfloat16)


def draw_q_gain(key, part):
    key = jax.random.fold_in(key, 5)
    return jnp.exp(jax.random.uniform(key, (D_HEAD,), jnp.float32, math.log(0.5), math.log(2.0)))


def draw_k_gain(key, part):
    key = jax.random.fold_in(key, 6)
    return jnp.exp(jax.random.uniform(key, (D_HEAD,), jnp.float32, math.log(0.5), math.log(2.0)))


def draw_mean_codes(key, part):
    key = jax.random.fold_in(key, 7)
    code_shape = (CLIPS, SEQ_LEN, HEADS * D_HEAD)
    sign_bit = jax.random.randint(jax.random.fold_in(key, 1), code_shape, 0, 2)
    expo_field = jax.random.randint(jax.random.fold_in(key, 2), code_shape, 3, 10)
    mantissa = jax.random.randint(jax.random.fold_in(key, 3), code_shape, 0, 8)
    return (128 * sign_bit + 8 * expo_field + mantissa).astype(jnp.int32)


def draw_group_ids(key, part):
    key = jax.random.fold_in(key, 9)
    shuffled = jax.random.permutation(key, CLIPS)
    return (shuffled % GROUPS).astype(jnp.int32)


def place_ends(entries, rng, smallest, high):
    longest = entries.shape.index(max(entries.shape))
    spots = []
    for shift in (0, 1):
        where = [jax.random.randint(jax.random.fold_in(rng, axis), (), 0, length) for axis, length in enumerate(entries.shape)]
        where[longest] = (where[longest] + shift) % entries.shape[longest]
        spots.append(tuple(where))
    return entries.at[spots[0]].set(smallest).at[spots[1]].set(high)


def shard_levels(own_key, extent, cuts, smallest, top_value):
    level, own = 1.0, jax.random.fold_in(own_key, 6)
    for dim, shards_of in cuts:
        steps = jnp.exp(jax.random.uniform(jax.random.fold_in(own, dim), (shards_of,), jnp.float32, smallest / len(cuts), top_value / len(cuts)))
        level = level * jnp.repeat(steps, extent[dim] // shards_of).reshape([-1 if axis == dim else 1 for axis in range(len(extent))])
    return level


def normal_values(key, extent, scale, reach, pieces=(), held_as=jnp.bfloat16):
    values = scale * jax.random.normal(key, extent, jnp.float32)
    if pieces:
        values = values * shard_levels(key, extent, pieces, -0.22, 0.18)
    return jnp.clip(values, -reach, reach).astype(held_as)


def setup_inputs(seed: int = 0) -> dict:
    streams_of = jax.random.split(jax.random.key(seed), 12)
    query = draw_query(jax.random.fold_in(streams_of[11], 71), 0)
    key = draw_key(jax.random.fold_in(streams_of[11], 71), 0)
    value = normal_values(streams_of[2], (CLIPS, SEQ_LEN, HEADS * D_HEAD), 1.0, 6.0, ((0, 16), (1, 16)))
    q_gain = draw_q_gain(jax.random.fold_in(streams_of[11], 71), 0)
    k_gain = draw_k_gain(jax.random.fold_in(streams_of[11], 71), 0)
    noise = normal_values(streams_of[5], (CLIPS, SEQ_LEN, HEADS * D_HEAD), 1.0, 5.0, ((0, 16), (1, 16)))
    mean_codes = draw_mean_codes(jax.random.fold_in(streams_of[11], 71), 0)
    scale_exps = place_ends(jax.random.randint(streams_of[7], (CLIPS, SEQ_LEN, HEADS), -2, 2), jax.random.fold_in(streams_of[7], 1), -2, 1).astype(jnp.int32)
    step_index = place_ends(jax.random.randint(streams_of[8], (CLIPS,), 1, STEPS), jax.random.fold_in(streams_of[8], 1), 1, STEPS - 1).astype(jnp.int32)
    rewards = normal_values(streams_of[9], (CLIPS,), 1.0, 4.0, (), jnp.float32)
    group_ids = draw_group_ids(jax.random.fold_in(streams_of[11], 71), 0)
    return dict(query=query, key=key, value=value, q_gain=q_gain, k_gain=k_gain, noise=noise, mean_codes=mean_codes, scale_exps=scale_exps, step_index=step_index, rewards=rewards, group_ids=group_ids)


EPS = 1e-06

def decode_means(codes, exponents):
    sign_bit = (codes // 128).astype(jnp.float32)
    expo_field = (codes // 8 % 16).astype(jnp.float32)
    mantissa = (codes % 8).astype(jnp.float32)
    magnitude = (1.0 + mantissa / 8.0) * jnp.exp2(expo_field - 7.0)
    scaled = magnitude * (1.0 - 2.0 * sign_bit) * jnp.exp2(exponents.astype(jnp.float32))[..., None]
    return scaled.astype(jnp.bfloat16)

def normalize(values, gain_vec):
    full_x = values.astype(jnp.float32)
    inv_rms = lax.rsqrt(lax.optimization_barrier(jnp.mean(full_x * full_x, axis=-1, keepdims=True)) + EPS)
    return ((gain_vec * full_x * inv_rms).astype(jnp.bfloat16), full_x, inv_rms)

def attend(q_norm, k_norm, v_heads):
    length, head_count, head_size = q_norm.shape
    block_rows = math.gcd(length, 512)
    scaling = 1.0 / math.sqrt(head_size)
    key_full = k_norm.astype(jnp.float32)
    value_full = v_heads.astype(jnp.float32)

    def block_attend(query_rows):
        scores = jnp.einsum('qhd,khd->hqk', query_rows.astype(jnp.float32), key_full) * scaling
        row_max = lax.optimization_barrier(jnp.max(scores, axis=-1, keepdims=True))
        log_total = row_max + jnp.log(lax.optimization_barrier(jnp.sum(jnp.exp(scores - row_max), axis=-1, keepdims=True)))
        attn_probs = jnp.exp(scores - log_total).astype(jnp.bfloat16)
        attn_probs = lax.optimization_barrier(attn_probs)
        result = jnp.einsum('hqk,khd->qhd', attn_probs.astype(jnp.float32), value_full)
        return (result.astype(jnp.bfloat16), jnp.transpose(log_total[:, :, 0]))
    attn_out, log_totals = lax.map(block_attend, q_norm.reshape(length // block_rows, block_rows, head_count, head_size))
    return (attn_out.reshape(length, head_count, head_size), log_totals.reshape(length, head_count))

def gradients(q_norm, k_norm, v_heads, log_total, grad_attn, delta_sum):
    length, head_count, head_size = q_norm.shape
    block_rows = math.gcd(length, 512)
    scaling = 1.0 / math.sqrt(head_size)
    query_full = q_norm.astype(jnp.float32)
    key_full = k_norm.astype(jnp.float32)
    value_full = v_heads.astype(jnp.float32)
    grad_full = grad_attn.astype(jnp.float32)

    def block_step(state_acc, index_now):
        value_acc, key_acc = state_acc
        row_start = index_now * block_rows
        query_rows = lax.dynamic_slice_in_dim(query_full, row_start, block_rows, 0)
        grad_rows = lax.dynamic_slice_in_dim(grad_full, row_start, block_rows, 0)
        total_rows = lax.dynamic_slice_in_dim(log_total, row_start, block_rows, 0)
        delta_rows = lax.dynamic_slice_in_dim(delta_sum, row_start, block_rows, 0)
        scores = jnp.einsum('qhd,khd->hqk', query_rows, key_full) * scaling
        attn_probs = jnp.exp(scores - jnp.transpose(total_rows)[:, :, None])
        probs_low = lax.optimization_barrier(attn_probs.astype(jnp.bfloat16))
        value_acc = value_acc + jnp.einsum('hqk,qhd->khd', probs_low.astype(jnp.float32), grad_rows)
        dprobs = jnp.einsum('qhd,khd->hqk', grad_rows, value_full)
        dscores = lax.optimization_barrier((attn_probs * (dprobs - jnp.transpose(delta_rows)[:, :, None])).astype(jnp.bfloat16))
        dscores = dscores.astype(jnp.float32)
        dquery = jnp.einsum('hqk,khd->qhd', dscores, key_full) * scaling
        key_acc = key_acc + jnp.einsum('hqk,qhd->khd', dscores, query_rows) * scaling
        return ((value_acc, key_acc), dquery)
    zero_acc = jnp.zeros((length, head_count, head_size), jnp.float32)
    (value_acc, key_acc), dquery = lax.scan(block_step, (zero_acc, zero_acc), jnp.arange(length // block_rows, dtype=jnp.int32))
    return (dquery.reshape(length, head_count, head_size), key_acc, value_acc)

def norm_back(full_x, inv_rms, gain_vec, grad_norm):
    scaled = gain_vec * grad_norm
    inner_sum = lax.optimization_barrier(jnp.sum(scaled * full_x, axis=-1, keepdims=True))
    grad_input = inv_rms * scaled - full_x * inv_rms * inv_rms * inv_rms * inner_sum / full_x.shape[-1]
    gain_part = lax.optimization_barrier(jnp.sum(grad_norm * full_x * inv_rms, axis=(0, 1)))
    return (grad_input.astype(jnp.bfloat16), gain_part)

def reference(query, key, value, q_gain, k_gain, noise, mean_codes, scale_exps, step_index, rewards, group_ids):
    same_group = (group_ids[:, None] == group_ids[None, :]).astype(jnp.float32)
    advantage = rewards - lax.optimization_barrier(jnp.sum(same_group * rewards[None, :], axis=1)) / lax.optimization_barrier(jnp.sum(same_group, axis=1))
    step_size = 1.0 / STEPS
    head_shape = (SEQ_LEN, HEADS, D_HEAD)
    flat_shape = (SEQ_LEN, HEADS * D_HEAD)

    def clip_pass(clip_items):
        query_c, key_c, value_c, noise_c, codes_c, exps_c, step_c, adv_c = clip_items
        q_norm, q_full, q_rinv = normalize(query_c.reshape(head_shape), q_gain)
        k_norm, k_full, k_rinv = normalize(key_c.reshape(head_shape), k_gain)
        v_heads = value_c.reshape(head_shape)
        attn_out, log_total = attend(q_norm, k_norm, v_heads)
        attn_out = lax.optimization_barrier(attn_out)
        old_mean = decode_means(codes_c.reshape(head_shape), exps_c)
        noise_level = 1.0 - step_c.astype(jnp.float32) / STEPS
        spread = 0.7 * jnp.sqrt(step_size * noise_level / (1.0 - noise_level))
        step_ratio = step_size / spread
        noise_full = noise_c.reshape(head_shape).astype(jnp.float32)
        mean_shift = step_ratio * (attn_out.astype(jnp.float32) - old_mean.astype(jnp.float32))
        log_ratio = -lax.optimization_barrier(jnp.sum(2.0 * noise_full * mean_shift + mean_shift * mean_shift, axis=(1, 2))) / (2.0 * HEADS * D_HEAD)
        weight = adv_c * jnp.exp(log_ratio) * step_ratio
        grad_attn = lax.optimization_barrier((weight[:, None, None] * (noise_full + mean_shift)).astype(jnp.bfloat16))
        delta_sum = lax.optimization_barrier(jnp.sum(grad_attn.astype(jnp.float32) * attn_out.astype(jnp.float32), axis=-1))
        grad_qn, grad_kn, grad_vh = gradients(q_norm, k_norm, v_heads, log_total, grad_attn, delta_sum)
        grad_q, q_part = norm_back(q_full, q_rinv, q_gain, grad_qn)
        grad_k, k_part = norm_back(k_full, k_rinv, k_gain, grad_kn)
        return (grad_q.reshape(flat_shape), grad_k.reshape(flat_shape), grad_vh.astype(jnp.bfloat16).reshape(flat_shape), q_part, k_part)
    grad_q, grad_k, grad_v, q_parts, k_parts = lax.map(clip_pass, (query, key, value, noise, mean_codes, scale_exps, step_index, advantage))
    factor = 1.0 / math.sqrt(CLIPS * SEQ_LEN * HEADS)
    return (grad_q, grad_k, grad_v, lax.optimization_barrier(jnp.sum(q_parts, axis=0)) * factor, lax.optimization_barrier(jnp.sum(k_parts, axis=0)) * factor)
```

```python
import functools
import math

import jax
import jax.numpy as jnp
from jax import lax
from jax.experimental import pallas as pl
from jax.experimental.pallas import tpu as pltpu
from jax.sharding import PartitionSpec as P

MESH = pl.DeviceIdType.MESH
F32 = jnp.float32
BF16 = jnp.bfloat16
STEPS = 10
EPS = 1e-6
NY, NZ = 2, 8
DZ = (0, 1, 7, 2, 6, 3, 5, 4)
BACK = (0, 2, 1, 4, 3, 6, 5, 7)
TOK, D = 128, 128
ROWS = 2048
CHUNKS = 2
TC = TOK // CHUNKS
RC = ROWS // CHUNKS
TILE = 256
GROUPS = RC // 128
SCALE = 1.0 / math.sqrt(D)
LOG2E = math.log2(math.e)

KINDS = ("k", "q0", "q1", "v", "u0", "u1", "w0", "w1", "dq0", "dq1", "dv", "dk", "gd", "gs")
ROW = {name: i for i, name in enumerate(KINDS)}


def ring_step(t):
    odd = lax.rem(t, 2)
    return lax.rem(odd * ((t + 1) // 2) + (1 - odd) * (NZ - t // 2), NZ)


def dot(a, b, dims):
    return lax.dot_general(a, b, (dims, ((), ())), preferred_element_type=F32)


def kernel(
    q_in, k_in, v_in, noise_in, codes_in, exps_in, qg_ref, kg_ref, step_ref, rew_ref, gid_ref,
    dq_out, dk_out, dv_out, gq_out, gk_out,
    k_buf, v_buf, q_buf, u_buf, u_src, noise_v, codes_v, exps_v,
    kn, qn, qn_t, attn, d_t, g_nat, g_t, probs, probs_b, ds, dq_buf, dk_buf, dv_buf,
    nsq, part, parts, weights, gain_src, gains, gain_src2, gains2,
    load_sem, self_sem, send_sem, recv_sem,
):
    me = lax.axis_index("seq")
    clip = lax.axis_index("dp")
    y, z = me // NZ, lax.rem(me, NZ)

    def at(m, yy):
        return yy * NZ + lax.rem(z + DZ[m], NZ)

    def others():
        yield 1 - y, (1 - y) * NZ + z, y
        for m in range(1, NZ):
            for yy in range(NY):
                yield 2 * m + yy, at(m, yy), 2 * BACK[m] + y

    def remote(kind, src, dst, peer, slot):
        return pltpu.make_async_remote_copy(
            src_ref=src, dst_ref=dst, send_sem=send_sem.at[ROW[kind], slot],
            recv_sem=recv_sem.at[ROW[kind], me], device_id={"seq": peer}, device_id_type=MESH,
        )

    def await_from(kind, dst, peer):
        pltpu.make_async_remote_copy(
            src_ref=dst, dst_ref=dst, send_sem=send_sem.at[ROW[kind], 0],
            recv_sem=recv_sem.at[ROW[kind], peer], device_id={"seq": peer}, device_id_type=MESH,
        ).wait_recv()

    loads = [
        pltpu.make_async_copy(noise_in.at[0], noise_v, load_sem.at[0]),
        pltpu.make_async_copy(codes_in.at[0], codes_v, load_sem.at[1]),
        pltpu.make_async_copy(exps_in.at[0], exps_v, load_sem.at[2]),
    ]
    for c in loads:
        c.start()

    barrier = pltpu.get_barrier_semaphore()
    for _, peer, _ in others():
        pl.semaphore_signal(barrier, inc=1, device_id={"seq": peer}, device_id_type=MESH)
    for j in range(1, 16):
        pl.semaphore_signal(
            barrier, inc=1, device_id={"dp": lax.rem(clip + j, 16)}, device_id_type=MESH
        )
    pl.semaphore_wait(barrier, 30)

    sends = []
    selfs = []

    def own(src, dst, i):
        c = pltpu.make_async_copy(src, dst, self_sem.at[i])
        c.start()
        selfs.append(c)

    def cols(ref, head):
        return ref.at[0, :, pl.ds(pl.multiple_of(head * D, D), D)]

    def piece(ref, head, c):
        return ref.at[0, pl.ds(c * TC, TC), pl.ds(pl.multiple_of(head * D, D), D)]

    def send(kind, src, dst, peer, slot):
        c = remote(kind, src, dst, peer, slot)
        c.start()
        sends.append(c)

    for slot, peer, there in others():
        send("k", cols(k_in, peer), k_buf.at[there], peer, slot)
    own(cols(k_in, me), k_buf.at[y], 0)
    for c in range(CHUNKS):
        for slot, peer, there in others():
            send("q%d" % c, piece(q_in, peer, c), q_buf.at[c, there], peer, slot)
        own(piece(q_in, me, c), q_buf.at[c, y], 1 + c)
    for slot, peer, there in others():
        send("v", cols(v_in, peer), v_buf.at[there], peer, slot)
    own(cols(v_in, me), v_buf.at[y], 3)

    level = 1.0 - jnp.broadcast_to(step_ref[...].astype(F32), (1, 128)) / STEPS
    step_size = 1.0 / STEPS
    ratio = step_size / (0.7 * jnp.sqrt(step_size * level / (1.0 - level)))
    gid = gid_ref[...].astype(F32)
    rewards = rew_ref[...]
    picked = (lax.broadcasted_iota(jnp.int32, gid.shape, 1) == clip).astype(F32)
    own_gid = jnp.sum(picked * gid, axis=1, keepdims=True)
    same = (gid == own_gid).astype(F32)
    advantage = jnp.sum(picked * rewards, axis=1, keepdims=True) - jnp.sum(
        same * rewards, axis=1, keepdims=True
    ) / jnp.sum(same, axis=1, keepdims=True)

    for c in loads:
        c.wait()
    scales = jnp.exp2(exps_v[...].astype(F32))
    noise_sq = jnp.zeros((TOK, D), F32)
    for h in range(16):
        code = codes_v[:, h * D:(h + 1) * D]
        magnitude = ((8 + (code & 7)) << ((code >> 3) & 15)).astype(F32) * (1.0 / 1024.0)
        old = jnp.where(code >= 128, -magnitude, magnitude) * scales[:, h:h + 1]
        noise = noise_v[:, h * D:(h + 1) * D].astype(F32)
        u_src[h] = (noise - ratio * old.astype(BF16).astype(F32)).astype(BF16)
        noise_sq = noise_sq + noise * noise
    nsq[...] = jnp.sum(jnp.transpose(noise_sq), axis=0, keepdims=True)

    for c in range(CHUNKS):
        for slot, peer, there in others():
            send("u%d" % c, u_src.at[peer, pl.ds(c * TC, TC)], u_buf.at[c, there], peer, slot)
        own(u_src.at[me, pl.ds(c * TC, TC)], u_buf.at[c, y], 4 + c)

    def normed(x, gain):
        rinv = lax.rsqrt(jnp.mean(x * x, axis=1, keepdims=True) + EPS)
        return (gain * x * rinv).astype(BF16)

    for slot, peer, _ in others():
        await_from("k", k_buf.at[slot], peer)
    selfs[0].wait()

    @pl.loop(0, 16)
    def _(n):
        kn[pl.ds(pl.multiple_of(n * D, D), D), :] = normed(k_buf[n].astype(F32), kg_ref[...])

    for c in range(CHUNKS):
        for slot, peer, _ in others():
            await_from("q%d" % c, q_buf.at[c, slot], peer)
        selfs[1 + c].wait()

    def block(ref, g):
        c, m = g // GROUPS, lax.rem(g, GROUPS)
        return ref[c, pl.ds(m * CHUNKS, CHUNKS)].reshape(128, D)

    def rows_of(g, size=128):
        return pl.ds(pl.multiple_of(g * size, size), size)

    @pl.loop(0, 16)
    def _(g):
        x = normed(block(q_buf, g).astype(F32), qg_ref[...])
        qn[rows_of(g), :] = x
        qn_t[:, rows_of(g)] = jnp.transpose(x.astype(F32)).astype(BF16)

    @pl.loop(0, ROWS // TILE)
    def _(i):
        rows = rows_of(i, TILE)
        s = dot(qn[rows, :], kn[...], ((1,), (1,)))
        e = jnp.exp2((s - jnp.max(s, axis=1, keepdims=True)) * (SCALE * LOG2E))
        p = e * (1.0 / jnp.sum(e, axis=1, keepdims=True))
        probs[rows, :] = p
        probs_b[rows, :] = p.astype(BF16)

    for slot, peer, _ in others():
        await_from("v", v_buf.at[slot], peer)
    selfs[3].wait()

    def values():
        return v_buf[...].reshape(ROWS, D)

    @pl.loop(0, ROWS // TILE)
    def _(i):
        rows = rows_of(i, TILE)
        attn[rows, :] = dot(probs_b[rows, :], values(), ((1,), (0,))).astype(BF16)

    for c in range(CHUNKS):
        for slot, peer, _ in others():
            await_from("u%d" % c, u_buf.at[c, slot], peer)
        selfs[4 + c].wait()

        @pl.loop(0, GROUPS)
        def _(m, c=c):
            g = c * GROUPS + m
            rows = rows_of(g)
            x = block(u_buf, g).astype(F32) + ratio * attn[rows, :].astype(F32)
            x_t = jnp.transpose(x)
            d_t[:, rows] = x_t
            part[c, pl.ds(lax.rem(z + ring_step(m), NZ), 1), :] = jnp.sum(
                x_t * x_t, axis=0, keepdims=True
            )

        line = nsq[...]
        halves = jnp.where(y == c, line, jnp.concatenate([line[:, TC:], line[:, :TC]], axis=1))
        shape = (GROUPS, 128)
        here = (lax.broadcasted_iota(jnp.int32, shape, 0) == z) & (
            lax.broadcasted_iota(jnp.int32, shape, 1) // TC == y
        )
        mine = part[c] - jnp.where(here, jnp.broadcast_to(halves, shape), 0.0)
        part[c] = mine
        parts[c, me] = mine
        for slot, peer, _ in others():
            send("w%d" % c, part.at[c], parts.at[c, me], peer, slot)

    def weigh(c):
        for slot, peer, _ in others():
            await_from("w%d" % c, parts.at[c, peer], peer)
        total = jnp.sum(parts[c], axis=0)
        weights[c] = advantage * jnp.exp(total * (-1.0 / (2.0 * ROWS))) * ratio

    def weigh_blocks(c):
        @pl.loop(0, GROUPS)
        def _(m):
            rows = rows_of(c * GROUPS + m)
            w = weights[c, pl.ds(lax.rem(z + ring_step(m), NZ), 1), :]
            x = w * d_t[:, rows]
            g_t[:, rows] = x.astype(BF16)
            g_nat[rows, :] = jnp.transpose(x).astype(BF16)

    def out_copy(kind, src, dst, peer, slot):
        @pl.when(peer != me)
        def _():
            remote(kind, src, dst, peer, slot).start()

        @pl.when(peer == me)
        def _():
            pltpu.make_async_copy(src, dst, self_sem.at[6 + ROW[kind] - ROW["dq0"]]).start()

    def own_cols(ref):
        return ref.at[0, :, pl.ds(pl.multiple_of(me * D, D), D)]

    def own_piece(ref, c):
        return ref.at[0, pl.ds(c * TC, TC), pl.ds(pl.multiple_of(me * D, D), D)]

    def norm_back(x, gain, grad):
        rinv = lax.rsqrt(jnp.mean(x * x, axis=1, keepdims=True) + EPS)
        scaled = gain * grad
        inner = jnp.sum(scaled * x, axis=1, keepdims=True)
        out = rinv * scaled - x * (rinv * rinv * rinv * inner * (1.0 / D))
        return out.astype(BF16), jnp.sum(grad * x * rinv, axis=0, keepdims=True)

    def backward_rows(c):
        @pl.loop(0, RC // TILE)
        def _(i):
            rows = rows_of(c * (RC // TILE) + i, TILE)
            g = g_nat[rows, :]
            delta = jnp.sum(g.astype(F32) * attn[rows, :].astype(F32), axis=1, keepdims=True)
            dp = dot(g, values(), ((1,), (1,)))
            ds[rows, :] = (probs[rows, :] * (dp - delta)).astype(BF16)

    per_tile = TILE // TC

    def query_rows(c):
        @pl.loop(0, RC // TILE)
        def _(i):
            rows = rows_of(c * (RC // TILE) + i, TILE)
            grad = dot(ds[rows, :], kn[...], ((1,), (0,))) * SCALE
            x = q_buf[c, pl.ds(i * per_tile, per_tile)].reshape(TILE, D).astype(F32)
            out, gain = norm_back(x, qg_ref[...], grad)
            dq_buf[c, pl.ds(i * per_tile, per_tile)] = out.reshape(per_tile, TC, D)
            gain_src[0:1, :] = gain_src[0:1, :] + gain
            for j in range(per_tile):
                slot = i * per_tile + j
                peer = (j % NY) * NZ + lax.rem(z + ring_step(slot // 2), NZ)
                out_copy("dq%d" % c, dq_buf.at[c, slot], own_piece(dq_out, c), peer, slot)

    gain_src[...] = jnp.zeros_like(gain_src)

    weigh(0)
    weigh_blocks(0)
    backward_rows(0)
    query_rows(0)
    weigh(1)
    weigh_blocks(1)

    @pl.loop(0, NZ)
    def _(t):
        wide = rows_of(t, 256)
        acc = dot(g_t[...], probs_b[:, wide], ((1,), (0,)))
        for j in range(NY):
            slot = t * NY + j
            dv_buf[slot] = jnp.transpose(acc[:, j * D:(j + 1) * D]).astype(BF16)
            peer = j * NZ + lax.rem(z + ring_step(t), NZ)
            out_copy("dv", dv_buf.at[slot], own_cols(dv_out), peer, slot)

    backward_rows(1)

    @pl.loop(0, NZ)
    def _(t):
        wide = rows_of(t, 256)
        acc = dot(qn_t[...], ds[:, wide], ((1,), (0,)))
        for j in range(NY):
            slot = t * NY + j
            grad = jnp.transpose(acc[:, j * D:(j + 1) * D]) * SCALE
            out, gain = norm_back(k_buf[slot].astype(F32), kg_ref[...], grad)
            dk_buf[slot] = out
            gain_src[1:2, :] = gain_src[1:2, :] + gain
            peer = j * NZ + lax.rem(z + ring_step(t), NZ)
            out_copy("dk", dk_buf.at[slot], own_cols(dk_out), peer, slot)

    query_rows(1)

    gains[clip] = gain_src[...]
    for j in range(1, 16):
        c = pltpu.make_async_remote_copy(
            src_ref=gain_src, dst_ref=gains.at[clip], send_sem=send_sem.at[ROW["gd"], j],
            recv_sem=recv_sem.at[ROW["gd"], clip], device_id={"dp": lax.rem(clip + j, 16)},
            device_id_type=MESH,
        )
        c.start()
        sends.append(c)
    for j in range(1, 16):
        peer = lax.rem(clip + j, 16)
        pltpu.make_async_remote_copy(
            src_ref=gain_src, dst_ref=gains.at[peer], send_sem=send_sem.at[ROW["gd"], 0],
            recv_sem=recv_sem.at[ROW["gd"], peer], device_id={"dp": peer}, device_id_type=MESH,
        ).wait_recv()
    total = jnp.sum(gains[...], axis=0)
    gain_src2[...] = total
    gains2[me] = total
    for slot, peer, _ in others():
        send("gs", gain_src2, gains2.at[me], peer, slot)
    for slot, peer, _ in others():
        await_from("gs", gains2.at[peer], peer)
    total = jnp.sum(gains2[...], axis=0) * (1.0 / math.sqrt(16.0 * 16.0 * ROWS))
    gq_out[...] = total[0:1, :]
    gk_out[...] = total[1:2, :]

    for kind, out in (("dv", dv_out), ("dk", dk_out)):
        for slot, peer, _ in others():
            await_from(kind, own_cols(out), peer)
    for c in range(CHUNKS):
        for slot, peer, _ in others():
            await_from("dq%d" % c, own_piece(dq_out, c), peer)
    for kind, src, dst in (
        ("dq0", dq_buf.at[0, y], own_piece(dq_out, 0)), ("dq1", dq_buf.at[1, y], own_piece(dq_out, 1)),
        ("dv", dv_buf.at[y], own_cols(dv_out)), ("dk", dk_buf.at[y], own_cols(dk_out)),
    ):
        pltpu.make_async_copy(src, dst, self_sem.at[6 + ROW[kind] - ROW["dq0"]]).wait()
        for slot, peer, _ in others():
            remote(kind, src, dst, peer, slot).wait_send()
    for c in sends:
        c.wait_send()


def per_device(q, k, v, q_gain, k_gain, noise, codes, exps, step, rewards, gids):
    hbm, vmem = pl.BlockSpec(memory_space=pl.ANY), pl.BlockSpec(memory_space=pltpu.VMEM)
    big = jax.ShapeDtypeStruct((1, TOK, 16 * D), BF16)
    row = jax.ShapeDtypeStruct((1, D), F32)
    dma = pltpu.SemaphoreType.DMA
    halves = (CHUNKS, 16, TC, D)
    dq, dk, dv, gq, gk = pl.pallas_call(
        kernel,
        out_shape=(big, big, big, row, row),
        in_specs=[hbm] * 6 + [vmem] * 5,
        out_specs=(hbm, hbm, hbm, vmem, vmem),
        scratch_shapes=[
            pltpu.VMEM((16, TOK, D), BF16),
            pltpu.VMEM((16, TOK, D), BF16),
            pltpu.VMEM(halves, BF16),
            pltpu.VMEM(halves, BF16),
            pltpu.VMEM((16, TOK, D), BF16),
            pltpu.VMEM((TOK, 16 * D), BF16),
            pltpu.VMEM((TOK, 16 * D), jnp.int32),
            pltpu.VMEM((TOK, 16), jnp.int32),
            pltpu.VMEM((ROWS, D), BF16),
            pltpu.VMEM((ROWS, D), BF16),
            pltpu.VMEM((D, ROWS), BF16),
            pltpu.VMEM((ROWS, D), BF16),
            pltpu.VMEM((D, ROWS), F32),
            pltpu.VMEM((ROWS, D), BF16),
            pltpu.VMEM((D, ROWS), BF16),
            pltpu.VMEM((ROWS, ROWS), F32),
            pltpu.VMEM((ROWS, ROWS), BF16),
            pltpu.VMEM((ROWS, ROWS), BF16),
            pltpu.VMEM(halves, BF16),
            pltpu.VMEM((16, TOK, D), BF16),
            pltpu.VMEM((16, TOK, D), BF16),
            pltpu.VMEM((1, 128), F32),
            pltpu.VMEM((CHUNKS, GROUPS, 128), F32),
            pltpu.VMEM((CHUNKS, 16, GROUPS, 128), F32),
            pltpu.VMEM((CHUNKS, GROUPS, 128), F32),
            pltpu.VMEM((8, 128), F32),
            pltpu.VMEM((16, 8, 128), F32),
            pltpu.VMEM((8, 128), F32),
            pltpu.VMEM((16, 8, 128), F32),
            dma((3,)),
            dma((10,)),
            dma((len(KINDS), 16)),
            dma((len(KINDS), 16)),
        ],
        compiler_params=pltpu.CompilerParams(
            collective_id=0, has_side_effects=True, vmem_limit_bytes=58 * 2**20
        ),
    )(
        q, k, v, noise, codes, exps, q_gain.reshape(1, D), k_gain.reshape(1, D),
        step.reshape(1, 1), rewards.reshape(1, 16), gids.reshape(1, 16),
    )
    return dq, dk, dv, gq.reshape(D), gk.reshape(D)


def solution(mesh):
    tokens = P("dp", "seq", None)
    return jax.shard_map(
        per_device,
        mesh=mesh,
        in_specs=(
            tokens, tokens, tokens, P(), P(), tokens, tokens, tokens, P("dp"), P(), P(),
        ),
        out_specs=(tokens, tokens, tokens, P(), P()),
        check_vma=False,
    )
```

```python
import functools
import math

import jax
import jax.numpy as jnp
from jax import lax
from jax.experimental import pallas as pl
from jax.experimental.pallas import tpu as pltpu
from jax.sharding import PartitionSpec as P

MESH = pl.DeviceIdType.MESH
F32 = jnp.float32
BF16 = jnp.bfloat16
STEPS = 10
EPS = 1e-6
NY, NZ = 2, 8
DZ = (0, 1, 7, 2, 6, 3, 5, 4)
BACK = (0, 2, 1, 4, 3, 6, 5, 7)
TOK, D = 128, 128
ROWS = 2048
CHUNKS = 2
TC = TOK // CHUNKS
RC = ROWS // CHUNKS
TILE = 256
GROUPS = RC // 128
SCALE = 1.0 / math.sqrt(D)
LOG2E = math.log2(math.e)

KINDS = ("k", "q", "v", "u0", "u1", "w0", "w1", "dq0", "dq1", "dv", "dk", "gd", "gs")
ROW = {name: i for i, name in enumerate(KINDS)}


def ring_step(t):
    odd = lax.rem(t, 2)
    return lax.rem(odd * ((t + 1) // 2) + (1 - odd) * (NZ - t // 2), NZ)


def dot(a, b, dims):
    return lax.dot_general(a, b, (dims, ((), ())), preferred_element_type=F32)


def kernel(
    q_in, k_in, v_in, noise_in, codes_in, exps_in, qg_ref, kg_ref, step_ref, rew_ref, gid_ref,
    dq_out, dk_out, dv_out, gq_out, gk_out,
    k_buf, v_buf, q_buf, u_buf, u_src, noise_v, codes_v, exps_v,
    kn, qn, qn_t, attn, d_t, g_nat, g_t, probs, probs_b, ds, dq_buf, dk_buf, dv_buf,
    nsq, part, parts, weights, gain_src, gains, gain_src2, gains2,
    load_sem, send_sem, recv_sem,
):
    me = lax.axis_index("seq")
    clip = lax.axis_index("dp")
    y, z = me // NZ, lax.rem(me, NZ)

    def at(m, yy):
        return yy * NZ + lax.rem(z + DZ[m], NZ)

    def others():
        yield (1 - y) * NZ + z, y
        for m in range(1, NZ):
            for yy in range(NY):
                yield at(m, yy), 2 * BACK[m] + y

    def remote(kind, src, dst, peer, axis="seq"):
        return pltpu.make_async_remote_copy(
            src_ref=src, dst_ref=dst, send_sem=send_sem.at[ROW[kind]], recv_sem=recv_sem.at[ROW[kind]],
            device_id={axis: peer}, device_id_type=MESH,
        )

    def send(kind, src, dst, peer, axis="seq"):
        remote(kind, src, dst, peer, axis).start()

    def own(kind, src, dst):
        pltpu.make_async_copy(src, dst, recv_sem.at[ROW[kind]]).start()

    def await_all(kind, ref):
        remote(kind, ref, ref, me).wait_recv()

    def await_sent(kind, ref):
        remote(kind, ref, ref, me).wait_send()

    loads = [
        pltpu.make_async_copy(noise_in.at[0], noise_v, load_sem.at[0]),
        pltpu.make_async_copy(codes_in.at[0], codes_v, load_sem.at[1]),
        pltpu.make_async_copy(exps_in.at[0], exps_v, load_sem.at[2]),
    ]
    for c in loads:
        c.start()

    barrier = pltpu.get_barrier_semaphore()
    for peer, _ in others():
        pl.semaphore_signal(barrier, inc=1, device_id={"seq": peer}, device_id_type=MESH)
    for j in range(1, 16):
        pl.semaphore_signal(
            barrier, inc=1, device_id={"dp": lax.rem(clip + j, 16)}, device_id_type=MESH
        )
    pl.semaphore_wait(barrier, 30)

    def cols(ref, head):
        return ref.at[0, :, pl.ds(pl.multiple_of(head * D, D), D)]

    def halves_of(ref, head):
        return ref.at[:, :, pl.ds(pl.multiple_of(head * D, D), D)]

    for peer, there in others():
        send("k", cols(k_in, peer), k_buf.at[there], peer)
    own("k", cols(k_in, me), k_buf.at[y])
    for peer, there in others():
        send("q", halves_of(q_in, peer), q_buf.at[:, there], peer)
    own("q", halves_of(q_in, me), q_buf.at[:, y])
    for peer, there in others():
        send("v", cols(v_in, peer), v_buf.at[there], peer)
    own("v", cols(v_in, me), v_buf.at[y])

    level = 1.0 - jnp.broadcast_to(step_ref[...].astype(F32), (1, 128)) / STEPS
    step_size = 1.0 / STEPS
    ratio = step_size / (0.7 * jnp.sqrt(step_size * level / (1.0 - level)))
    gid = gid_ref[...].astype(F32)
    rewards = rew_ref[...]
    picked = (lax.broadcasted_iota(jnp.int32, gid.shape, 1) == clip).astype(F32)
    own_gid = jnp.sum(picked * gid, axis=1, keepdims=True)
    same = (gid == own_gid).astype(F32)
    advantage = jnp.sum(picked * rewards, axis=1, keepdims=True) - jnp.sum(
        same * rewards, axis=1, keepdims=True
    ) / jnp.sum(same, axis=1, keepdims=True)

    for c in loads:
        c.wait()
    scales = jnp.transpose(jnp.exp2(exps_v[...].astype(F32)))
    noise_sq = jnp.zeros((TOK, D), F32)
    for h in range(16):
        code = codes_v[:, h * D:(h + 1) * D]
        magnitude = ((8 + (code & 7)) << ((code >> 3) & 15)).astype(F32) * (1.0 / 1024.0)
        old = jnp.where(code >= 128, -magnitude, magnitude) * scales[:, h:h + 1]
        noise = noise_v[:, h * D:(h + 1) * D].astype(F32)
        u_src[h] = (noise - ratio * old.astype(BF16).astype(F32)).astype(BF16)
        noise_sq = noise_sq + noise * noise
    nsq[...] = jnp.sum(jnp.transpose(noise_sq), axis=0, keepdims=True)

    def send_u(c):
        for peer, there in others():
            send("u%d" % c, u_src.at[peer, pl.ds(c * TC, TC)], u_buf.at[c, there], peer)
        own("u%d" % c, u_src.at[me, pl.ds(c * TC, TC)], u_buf.at[c, y])

    send_u(0)

    def normed(x, gain):
        rinv = lax.rsqrt(jnp.mean(x * x, axis=1, keepdims=True) + EPS)
        return (gain * x * rinv).astype(BF16)

    await_all("k", k_buf)

    @pl.loop(0, 16)
    def _(n):
        kn[pl.ds(pl.multiple_of(n * D, D), D), :] = normed(k_buf[n].astype(F32), kg_ref[...])

    await_all("q", q_buf)

    def block(ref, g):
        c, m = g // GROUPS, lax.rem(g, GROUPS)
        return ref[c, pl.ds(m * CHUNKS, CHUNKS)].reshape(128, D)

    def rows_of(g, size=128):
        return pl.ds(pl.multiple_of(g * size, size), size)

    @pl.loop(0, 16)
    def _(g):
        x = normed(block(q_buf, g).astype(F32), qg_ref[...])
        qn[rows_of(g), :] = x
        qn_t[:, rows_of(g)] = jnp.transpose(x.astype(F32)).astype(BF16)

    @pl.loop(0, ROWS // TILE)
    def _(i):
        rows = rows_of(i, TILE)
        s = dot(qn[rows, :], kn[...], ((1,), (1,)))
        e = jnp.exp2((s - jnp.max(s, axis=1, keepdims=True)) * (SCALE * LOG2E))
        p = e * (1.0 / jnp.sum(e, axis=1, keepdims=True))
        probs[rows, :] = p
        probs_b[rows, :] = p.astype(BF16)

    await_all("v", v_buf)

    def values():
        return v_buf[...].reshape(ROWS, D)

    @pl.loop(0, ROWS // TILE)
    def _(i):
        rows = rows_of(i, TILE)
        attn[rows, :] = dot(probs_b[rows, :], values(), ((1,), (0,))).astype(BF16)

    for c in range(CHUNKS):
        await_all("u%d" % c, u_buf.at[c])

        @pl.loop(0, GROUPS)
        def _(m, c=c):
            g = c * GROUPS + m
            rows = rows_of(g)
            x = block(u_buf, g).astype(F32) + ratio * attn[rows, :].astype(F32)
            x_t = jnp.transpose(x)
            d_t[:, rows] = x_t
            part[c, pl.ds(lax.rem(z + ring_step(m), NZ), 1), :] = jnp.sum(
                x_t * x_t, axis=0, keepdims=True
            )

        line = nsq[...]
        halves = jnp.where(y == c, line, jnp.concatenate([line[:, TC:], line[:, :TC]], axis=1))
        shape = (GROUPS, 128)
        here = (lax.broadcasted_iota(jnp.int32, shape, 0) == z) & (
            lax.broadcasted_iota(jnp.int32, shape, 1) // TC == y
        )
        mine = part[c] - jnp.where(here, jnp.broadcast_to(halves, shape), 0.0)
        part[c] = mine
        parts[c, me] = mine
        for peer, _ in others():
            send("w%d" % c, part.at[c], parts.at[c, me], peer)
        if c + 1 < CHUNKS:
            send_u(c + 1)

    def weigh(c):
        await_all("w%d" % c, parts.at[c, pl.ds(0, 15)])
        total = jnp.sum(parts[c], axis=0)
        weights[c] = advantage * jnp.exp(total * (-1.0 / (2.0 * ROWS))) * ratio

    def weigh_block(g):
        c, m = g // GROUPS, lax.rem(g, GROUPS)
        rows = rows_of(g)
        w = weights[c, pl.ds(lax.rem(z + ring_step(m), NZ), 1), :]
        x = w * d_t[:, rows]
        g_t[:, rows] = x.astype(BF16)
        g_nat[rows, :] = jnp.transpose(x).astype(BF16)

    def out_copy(kind, src, dst, peer):
        @pl.when(peer != me)
        def _():
            send(kind, src, dst, peer)

        @pl.when(peer == me)
        def _():
            own(kind, src, dst)

    def own_cols(ref):
        return ref.at[0, :, pl.ds(pl.multiple_of(me * D, D), D)]

    def own_piece(ref, c):
        return ref.at[0, pl.ds(c * TC, TC), pl.ds(pl.multiple_of(me * D, D), D)]

    def norm_back(x, gain, grad):
        rinv = lax.rsqrt(jnp.mean(x * x, axis=1, keepdims=True) + EPS)
        scaled = gain * grad
        inner = jnp.sum(scaled * x, axis=1, keepdims=True)
        out = rinv * scaled - x * (rinv * rinv * rinv * inner * (1.0 / D))
        return out.astype(BF16), jnp.sum(grad * x * rinv, axis=0, keepdims=True)

    def dscore_rows(i):
        rows = rows_of(i, TILE)
        g = g_nat[rows, :]
        delta = jnp.sum(g.astype(F32) * attn[rows, :].astype(F32), axis=1, keepdims=True)
        dp = dot(g, values(), ((1,), (1,)))
        ds[rows, :] = (probs[rows, :] * (dp - delta)).astype(BF16)

    per_tile = TILE // TC

    def query_rows(c, i):
        rows = rows_of(c * (RC // TILE) + i, TILE)
        grad = dot(ds[rows, :], kn[...], ((1,), (0,))) * SCALE
        x = q_buf[c, pl.ds(i * per_tile, per_tile)].reshape(TILE, D).astype(F32)
        out, gain = norm_back(x, qg_ref[...], grad)
        dq_buf[c, pl.ds(i * per_tile, per_tile)] = out.reshape(per_tile, TC, D)
        gain_src[0:1, :] = gain_src[0:1, :] + gain

    def send_query_rows(c, i):
        for j in range(per_tile):
            slot = i * per_tile + j
            peer = (j % NY) * NZ + lax.rem(z + ring_step(slot // 2), NZ)
            out_copy("dq%d" % c, dq_buf.at[c, slot], own_piece(dq_out, c), peer)

    gain_src[...] = jnp.zeros_like(gain_src)

    weigh(0)

    @pl.loop(0, RC // TILE)
    def _(i):
        for j in range(TILE // 128):
            weigh_block(i * (TILE // 128) + j)
        dscore_rows(i)
        query_rows(0, i)
        send_query_rows(0, i)

    weigh(1)

    @pl.loop(GROUPS, 2 * GROUPS)
    def _(g):
        weigh_block(g)

    @pl.loop(0, NZ)
    def _(t):
        wide = rows_of(t, 256)
        acc = dot(g_t[...], probs_b[:, wide], ((1,), (0,)))
        for j in range(NY):
            slot = t * NY + j
            dv_buf[slot] = jnp.transpose(acc[:, j * D:(j + 1) * D]).astype(BF16)
            peer = j * NZ + lax.rem(z + ring_step(t), NZ)
            out_copy("dv", dv_buf.at[slot], own_cols(dv_out), peer)

    @pl.loop(0, RC // TILE)
    def _(i):
        dscore_rows(RC // TILE + i)
        query_rows(1, i)

    @pl.loop(0, NZ)
    def _(t):
        wide = rows_of(t, 256)
        acc = dot(qn_t[...], ds[:, wide], ((1,), (0,)))
        for j in range(NY):
            slot = t * NY + j
            grad = jnp.transpose(acc[:, j * D:(j + 1) * D]) * SCALE
            out, gain = norm_back(k_buf[slot].astype(F32), kg_ref[...], grad)
            dk_buf[slot] = out
            gain_src[1:2, :] = gain_src[1:2, :] + gain

    gains[clip] = gain_src[...]
    for j in range(1, 16):
        send("gd", gain_src, gains.at[clip], lax.rem(clip + j, 16), "dp")

    @pl.loop(0, NZ)
    def _(t):
        for j in range(NY):
            slot = t * NY + j
            peer = j * NZ + lax.rem(z + ring_step(t), NZ)
            out_copy("dk", dk_buf.at[slot], own_cols(dk_out), peer)

    await_all("gd", gains.at[pl.ds(0, 15)])
    total = jnp.sum(gains[...], axis=0)
    gain_src2[...] = total
    gains2[me] = total
    for peer, _ in others():
        send("gs", gain_src2, gains2.at[me], peer)

    @pl.loop(0, RC // TILE)
    def _(i):
        send_query_rows(1, i)

    for kind, ref in (
        ("k", k_buf.at[pl.ds(0, 15)]), ("q", q_buf.at[:, pl.ds(0, 15)]), ("v", v_buf.at[pl.ds(0, 15)]),
        ("u0", u_buf.at[0, pl.ds(0, 15)]), ("u1", u_buf.at[1, pl.ds(0, 15)]),
        ("w0", parts.at[0, pl.ds(0, 15)]), ("w1", parts.at[1, pl.ds(0, 15)]),
        ("gd", gains.at[pl.ds(0, 15)]), ("gs", gains2.at[pl.ds(0, 15)]),
    ):
        await_sent(kind, ref)
    await_all("gs", gains2.at[pl.ds(0, 15)])
    total = jnp.sum(gains2[...], axis=0) * (1.0 / math.sqrt(16.0 * 16.0 * ROWS))
    gq_out[...] = total[0:1, :]
    gk_out[...] = total[1:2, :]

    for kind, buf, out in (
        ("dv", dv_buf.at[pl.ds(0, 15)], dv_out), ("dk", dk_buf.at[pl.ds(0, 15)], dk_out),
        ("dq0", dq_buf.at[0, pl.ds(0, 15)], dq_out.at[0, pl.ds(0, TC)]),
        ("dq1", dq_buf.at[1, pl.ds(0, 15)], dq_out.at[0, pl.ds(TC, TC)]),
    ):
        await_all(kind, out)
        await_sent(kind, buf)


def hand_over(*refs):
    for i in range(5):
        refs[5 + i][...] = refs[i][...]


def per_device(q, k, v, q_gain, k_gain, noise, codes, exps, step, rewards, gids):
    hbm, vmem = pl.BlockSpec(memory_space=pl.ANY), pl.BlockSpec(memory_space=pltpu.VMEM)
    big = jax.ShapeDtypeStruct((1, TOK, 16 * D), BF16)
    row = jax.ShapeDtypeStruct((1, D), F32)
    dma = pltpu.SemaphoreType.DMA
    halves = (CHUNKS, 16, TC, D)
    results = pl.pallas_call(
        kernel,
        out_shape=(big, big, big, row, row),
        in_specs=[hbm] * 6 + [vmem] * 5,
        out_specs=(hbm, hbm, hbm, vmem, vmem),
        scratch_shapes=[
            pltpu.VMEM((16, TOK, D), BF16),
            pltpu.VMEM((16, TOK, D), BF16),
            pltpu.VMEM(halves, BF16),
            pltpu.VMEM(halves, BF16),
            pltpu.VMEM((16, TOK, D), BF16),
            pltpu.VMEM((TOK, 16 * D), BF16),
            pltpu.VMEM((TOK, 16 * D), jnp.int32),
            pltpu.VMEM((16, TOK), jnp.int32),
            pltpu.VMEM((ROWS, D), BF16),
            pltpu.VMEM((ROWS, D), BF16),
            pltpu.VMEM((D, ROWS), BF16),
            pltpu.VMEM((ROWS, D), BF16),
            pltpu.VMEM((D, ROWS), F32),
            pltpu.VMEM((ROWS, D), BF16),
            pltpu.VMEM((D, ROWS), BF16),
            pltpu.VMEM((ROWS, ROWS), F32),
            pltpu.VMEM((ROWS, ROWS), BF16),
            pltpu.VMEM((ROWS, ROWS), BF16),
            pltpu.VMEM(halves, BF16),
            pltpu.VMEM((16, TOK, D), BF16),
            pltpu.VMEM((16, TOK, D), BF16),
            pltpu.VMEM((1, 128), F32),
            pltpu.VMEM((CHUNKS, GROUPS, 128), F32),
            pltpu.VMEM((CHUNKS, 16, GROUPS, 128), F32),
            pltpu.VMEM((CHUNKS, GROUPS, 128), F32),
            pltpu.VMEM((8, 128), F32),
            pltpu.VMEM((16, 8, 128), F32),
            pltpu.VMEM((8, 128), F32),
            pltpu.VMEM((16, 8, 128), F32),
            dma((3,)),
            dma((len(KINDS),)),
            dma((len(KINDS),)),
        ],
        compiler_params=pltpu.CompilerParams(
            collective_id=0, has_side_effects=True, vmem_limit_bytes=58 * 2**20
        ),
    )(
        q.reshape(CHUNKS, TC, 16 * D), k, v, noise, codes, jnp.swapaxes(exps, 1, 2), q_gain.reshape(1, D), k_gain.reshape(1, D),
        step.reshape(1, 1), rewards.reshape(1, 16), gids.reshape(1, 16),
    )
    dq, dk, dv, gq, gk = pl.pallas_call(
        hand_over,
        out_shape=(big, big, big, row, row),
        in_specs=[vmem] * 5,
        out_specs=(vmem,) * 5,
        compiler_params=pltpu.CompilerParams(vmem_limit_bytes=60 * 2**20),
    )(*results)
    return dq, dk, dv, gq.reshape(D), gk.reshape(D)


def solution(mesh):
    tokens = P("dp", "seq", None)
    return jax.shard_map(
        per_device,
        mesh=mesh,
        in_specs=(
            tokens, tokens, tokens, P(), P(), tokens, tokens, tokens, P("dp"), P(), P(),
        ),
        out_specs=(tokens, tokens, tokens, P(), P()),
        check_vma=False,
    )
```

```python
import functools
import math

import jax
import jax.numpy as jnp
from jax import lax
from jax.experimental import pallas as pl
from jax.experimental.pallas import tpu as pltpu
from jax.sharding import PartitionSpec as P

MESH = pl.DeviceIdType.MESH
F32 = jnp.float32
BF16 = jnp.bfloat16
STEPS = 10
EPS = 1e-6
NY, NZ = 2, 8
DZ = (0, 1, 7, 2, 6, 3, 5, 4)
BACK = (0, 2, 1, 4, 3, 6, 5, 7)
TOK, D = 128, 128
ROWS = 2048
CHUNKS = 2
TC = TOK // CHUNKS
RC = ROWS // CHUNKS
TILE = 256
GROUPS = RC // 128
SCALE = 1.0 / math.sqrt(D)
LOG2E = math.log2(math.e)
LEAD = 1

KINDS = ("k", "q", "v", "u0", "u1", "w0", "w1", "dq0", "dq1", "dv", "dk", "gs", "gd", "gt")
ROW = {name: i for i, name in enumerate(KINDS)}


def ring_step(t):
    odd = lax.rem(t, 2)
    return lax.rem(odd * ((t + 1) // 2) + (1 - odd) * (NZ - t // 2), NZ)


def dot(a, b, dims):
    return lax.dot_general(a, b, (dims, ((), ())), preferred_element_type=F32)


def kernel(
    q_in, k_in, v_in, noise_in, codes_in, exps_in, qg_ref, kg_ref, step_ref, rew_ref, gid_ref,
    dq_out, dk_out, dv_out, gq_out, gk_out,
    k_buf, v_buf, q_buf, u_buf, u_src, noise_v, codes_v, exps_v,
    kn, qn, qn_t, attn, d_t, g_nat, g_t, probs, probs_b, ds, dq_buf, dk_buf, dv_buf,
    nsq, part, parts, weights, gain_src, gains, gain_clip, gains2, gain_all,
    load_sem, send_sem, recv_sem,
):
    me = lax.axis_index("seq")
    clip = lax.axis_index("dp")
    y, z = me // NZ, lax.rem(me, NZ)

    def at(m, yy):
        return yy * NZ + lax.rem(z + DZ[m], NZ)

    def others():
        yield (1 - y) * NZ + z, y
        for m in range(1, NZ):
            for yy in range(NY):
                yield at(m, yy), 2 * BACK[m] + y

    def remote(kind, src, dst, peer, axis="seq"):
        return pltpu.make_async_remote_copy(
            src_ref=src, dst_ref=dst, send_sem=send_sem.at[ROW[kind]], recv_sem=recv_sem.at[ROW[kind]],
            device_id={axis: peer}, device_id_type=MESH,
        )

    def send(kind, src, dst, peer, axis="seq"):
        remote(kind, src, dst, peer, axis).start()

    def own(kind, src, dst):
        pltpu.make_async_copy(src, dst, recv_sem.at[ROW[kind]]).start()

    def await_all(kind, ref):
        remote(kind, ref, ref, me).wait_recv()

    def await_sent(kind, ref):
        remote(kind, ref, ref, me).wait_send()

    loads = [
        pltpu.make_async_copy(noise_in.at[0], noise_v, load_sem.at[0]),
        pltpu.make_async_copy(codes_in.at[0], codes_v, load_sem.at[1]),
        pltpu.make_async_copy(exps_in.at[0], exps_v, load_sem.at[2]),
    ]
    for c in loads:
        c.start()

    barrier = pltpu.get_barrier_semaphore()
    for peer, _ in others():
        pl.semaphore_signal(barrier, inc=1, device_id={"seq": peer}, device_id_type=MESH)

    @pl.when(me == LEAD)
    def _():
        for j in range(1, 16):
            pl.semaphore_signal(
                barrier, inc=1, device_id={"dp": lax.rem(clip + j, 16)}, device_id_type=MESH
            )
        pl.semaphore_wait(barrier, 30)

    @pl.when(me != LEAD)
    def _():
        pl.semaphore_wait(barrier, 15)

    def cols(ref, head):
        return ref.at[0, :, pl.ds(pl.multiple_of(head * D, D), D)]

    def halves_of(ref, head):
        return ref.at[:, :, pl.ds(pl.multiple_of(head * D, D), D)]

    for peer, there in others():
        send("k", cols(k_in, peer), k_buf.at[there], peer)
    own("k", cols(k_in, me), k_buf.at[y])
    for peer, there in others():
        send("q", halves_of(q_in, peer), q_buf.at[:, there], peer)
    own("q", halves_of(q_in, me), q_buf.at[:, y])
    for peer, there in others():
        send("v", cols(v_in, peer), v_buf.at[there], peer)
    own("v", cols(v_in, me), v_buf.at[y])

    level = 1.0 - jnp.broadcast_to(step_ref[...].astype(F32), (1, 128)) / STEPS
    step_size = 1.0 / STEPS
    ratio = step_size / (0.7 * jnp.sqrt(step_size * level / (1.0 - level)))
    gid = gid_ref[...].astype(F32)
    rewards = rew_ref[...]
    picked = (lax.broadcasted_iota(jnp.int32, gid.shape, 1) == clip).astype(F32)
    own_gid = jnp.sum(picked * gid, axis=1, keepdims=True)
    same = (gid == own_gid).astype(F32)
    advantage = jnp.sum(picked * rewards, axis=1, keepdims=True) - jnp.sum(
        same * rewards, axis=1, keepdims=True
    ) / jnp.sum(same, axis=1, keepdims=True)

    for c in loads:
        c.wait()
    scales = jnp.transpose(jnp.exp2(exps_v[...].astype(F32)))
    noise_sq = jnp.zeros((TOK, D), F32)
    for h in range(16):
        code = codes_v[:, h * D:(h + 1) * D]
        magnitude = ((8 + (code & 7)) << ((code >> 3) & 15)).astype(F32) * (1.0 / 1024.0)
        old = jnp.where(code >= 128, -magnitude, magnitude) * scales[:, h:h + 1]
        noise = noise_v[:, h * D:(h + 1) * D].astype(F32)
        u_src[h] = (noise - ratio * old.astype(BF16).astype(F32)).astype(BF16)
        noise_sq = noise_sq + noise * noise
    nsq[...] = jnp.sum(jnp.transpose(noise_sq), axis=0, keepdims=True)

    def send_u(c):
        rows = pl.ds(c * TC, TC)
        for peer, there in others():
            send("u%d" % c, u_src.at[peer, rows], u_buf.at[c, there], peer)
        own("u%d" % c, u_src.at[me, rows], u_buf.at[c, y])

    send_u(0)
    send_u(1)

    def normed(x, gain):
        rinv = lax.rsqrt(jnp.mean(x * x, axis=1, keepdims=True) + EPS)
        return (gain * x * rinv).astype(BF16)

    await_all("k", k_buf)

    @pl.loop(0, 16)
    def _(n):
        kn[pl.ds(pl.multiple_of(n * D, D), D), :] = normed(k_buf[n].astype(F32), kg_ref[...])

    await_all("q", q_buf)

    def block(ref, g):
        c, m = g // GROUPS, lax.rem(g, GROUPS)
        return ref[c, pl.ds(m * CHUNKS, CHUNKS)].reshape(128, D)

    def rows_of(g, size=128):
        return pl.ds(pl.multiple_of(g * size, size), size)

    @pl.loop(0, 16)
    def _(g):
        x = normed(block(q_buf, g).astype(F32), qg_ref[...])
        qn[rows_of(g), :] = x
        qn_t[:, rows_of(g)] = jnp.transpose(x.astype(F32)).astype(BF16)

    @pl.loop(0, ROWS // TILE)
    def _(i):
        rows = rows_of(i, TILE)
        s = dot(qn[rows, :], kn[...], ((1,), (1,)))
        e = jnp.exp2((s - jnp.max(s, axis=1, keepdims=True)) * (SCALE * LOG2E))
        p = e * (1.0 / jnp.sum(e, axis=1, keepdims=True))
        probs[rows, :] = p
        probs_b[rows, :] = p.astype(BF16)

    await_all("v", v_buf)

    def values():
        return v_buf[...].reshape(ROWS, D)

    @pl.loop(0, ROWS // TILE)
    def _(i):
        rows = rows_of(i, TILE)
        attn[rows, :] = dot(probs_b[rows, :], values(), ((1,), (0,))).astype(BF16)

    for c in range(CHUNKS):
        await_all("u%d" % c, u_buf.at[c])

        @pl.loop(0, GROUPS)
        def _(m, c=c):
            g = c * GROUPS + m
            rows = rows_of(g)
            x = block(u_buf, g).astype(F32) + ratio * attn[rows, :].astype(F32)
            x_t = jnp.transpose(x)
            d_t[:, rows] = x_t
            part[c, pl.ds(lax.rem(z + ring_step(m), NZ), 1), :] = jnp.sum(
                x_t * x_t, axis=0, keepdims=True
            )

        line = nsq[...]
        halves = jnp.where(y == c, line, jnp.concatenate([line[:, TC:], line[:, :TC]], axis=1))
        shape = (GROUPS, 128)
        here = (lax.broadcasted_iota(jnp.int32, shape, 0) == z) & (
            lax.broadcasted_iota(jnp.int32, shape, 1) // TC == y
        )
        mine = part[c] - jnp.where(here, jnp.broadcast_to(halves, shape), 0.0)
        part[c] = mine
        parts[c, me] = mine
        for peer, _ in others():
            send("w%d" % c, part.at[c], parts.at[c, me], peer)

    def weigh(c):
        await_all("w%d" % c, parts.at[c, pl.ds(0, 15)])
        total = jnp.sum(parts[c], axis=0)
        weights[c] = advantage * jnp.exp(total * (-1.0 / (2.0 * ROWS))) * ratio

    def weigh_block(g):
        c, m = g // GROUPS, lax.rem(g, GROUPS)
        rows = rows_of(g)
        w = weights[c, pl.ds(lax.rem(z + ring_step(m), NZ), 1), :]
        x = w * d_t[:, rows]
        g_t[:, rows] = x.astype(BF16)
        g_nat[rows, :] = jnp.transpose(x).astype(BF16)

    def out_copy(kind, src, dst, peer):
        @pl.when(peer != me)
        def _():
            send(kind, src, dst, peer)

        @pl.when(peer == me)
        def _():
            own(kind, src, dst)

    def own_cols(ref):
        return ref.at[0, :, pl.ds(pl.multiple_of(me * D, D), D)]

    def own_piece(ref, c):
        return ref.at[0, pl.ds(c * TC, TC), pl.ds(pl.multiple_of(me * D, D), D)]

    def norm_back(x, gain, grad):
        rinv = lax.rsqrt(jnp.mean(x * x, axis=1, keepdims=True) + EPS)
        scaled = gain * grad
        inner = jnp.sum(scaled * x, axis=1, keepdims=True)
        out = rinv * scaled - x * (rinv * rinv * rinv * inner * (1.0 / D))
        return out.astype(BF16), jnp.sum(grad * x * rinv, axis=0, keepdims=True)

    def dscore_rows(i):
        rows = rows_of(i, TILE)
        g = g_nat[rows, :]
        delta = jnp.sum(g.astype(F32) * attn[rows, :].astype(F32), axis=1, keepdims=True)
        dp = dot(g, values(), ((1,), (1,)))
        ds[rows, :] = (probs[rows, :] * (dp - delta)).astype(BF16)

    per_tile = TILE // TC

    def query_rows(c, i):
        rows = rows_of(c * (RC // TILE) + i, TILE)
        grad = dot(ds[rows, :], kn[...], ((1,), (0,))) * SCALE
        x = q_buf[c, pl.ds(i * per_tile, per_tile)].reshape(TILE, D).astype(F32)
        out, gain = norm_back(x, qg_ref[...], grad)
        dq_buf[c, pl.ds(i * per_tile, per_tile)] = out.reshape(per_tile, TC, D)
        gain_src[0:1, :] = gain_src[0:1, :] + gain

    def send_query_rows(c, i):
        for j in range(per_tile):
            slot = i * per_tile + j
            peer = (j % NY) * NZ + lax.rem(z + ring_step(slot // 2), NZ)
            out_copy("dq%d" % c, dq_buf.at[c, slot], own_piece(dq_out, c), peer)

    gain_src[...] = jnp.zeros_like(gain_src)

    weigh(0)

    @pl.loop(0, RC // TILE)
    def _(i):
        for j in range(TILE // 128):
            weigh_block(i * (TILE // 128) + j)
        dscore_rows(i)
        query_rows(0, i)
        send_query_rows(0, i)

    weigh(1)

    @pl.loop(GROUPS, 2 * GROUPS)
    def _(g):
        weigh_block(g)

    @pl.loop(0, NZ)
    def _(t):
        wide = rows_of(t, 256)
        acc = dot(g_t[...], probs_b[:, wide], ((1,), (0,)))
        for j in range(NY):
            slot = t * NY + j
            dv_buf[slot] = jnp.transpose(acc[:, j * D:(j + 1) * D]).astype(BF16)
            peer = j * NZ + lax.rem(z + ring_step(t), NZ)
            out_copy("dv", dv_buf.at[slot], own_cols(dv_out), peer)

    @pl.loop(0, RC // TILE)
    def _(i):
        dscore_rows(RC // TILE + i)
        query_rows(1, i)

    @pl.loop(0, NZ)
    def _(t):
        wide = rows_of(t, 256)
        acc = dot(qn_t[...], ds[:, wide], ((1,), (0,)))
        for j in range(NY):
            slot = t * NY + j
            grad = jnp.transpose(acc[:, j * D:(j + 1) * D]) * SCALE
            out, gain = norm_back(k_buf[slot].astype(F32), kg_ref[...], grad)
            dk_buf[slot] = out
            gain_src[1:2, :] = gain_src[1:2, :] + gain

    @pl.when(me != LEAD)
    def _():
        send("gs", gain_src, gains.at[me], LEAD)

    @pl.when(me == LEAD)
    def _():
        gains[me] = gain_src[...]

    def send_keys(first, last):
        @pl.loop(first, last)
        def _(t):
            for j in range(NY):
                slot = t * NY + j
                peer = j * NZ + lax.rem(z + ring_step(t), NZ)
                out_copy("dk", dk_buf.at[slot], own_cols(dk_out), peer)

    send_keys(0, NZ // 2)

    @pl.when(me == LEAD)
    def _():
        await_all("gs", gains.at[pl.ds(0, 15)])
        total = jnp.sum(gains[...], axis=0)
        gain_clip[...] = total
        gains2[clip] = total
        for j in range(1, 16):
            send("gd", gain_clip, gains2.at[clip], lax.rem(clip + j, 16), "dp")

    send_keys(NZ // 2, NZ)

    @pl.loop(0, RC // TILE - 1)
    def _(i):
        send_query_rows(1, i)

    @pl.when(me == LEAD)
    def _():
        await_all("gd", gains2.at[pl.ds(0, 15)])
        gain_all[...] = jnp.sum(gains2[...], axis=0) * (1.0 / math.sqrt(16.0 * 16.0 * ROWS))
        for peer, _ in others():
            send("gt", gain_all, gain_all, peer)

    send_query_rows(1, RC // TILE - 1)

    for kind, ref in (
        ("k", k_buf.at[pl.ds(0, 15)]), ("q", q_buf.at[:, pl.ds(0, 15)]), ("v", v_buf.at[pl.ds(0, 15)]),
        ("u0", u_buf.at[0, pl.ds(0, 15)]), ("u1", u_buf.at[1, pl.ds(0, 15)]),
        ("w0", parts.at[0, pl.ds(0, 15)]), ("w1", parts.at[1, pl.ds(0, 15)]),
    ):
        await_sent(kind, ref)

    @pl.when(me == LEAD)
    def _():
        await_sent("gd", gains2.at[pl.ds(0, 15)])
        await_sent("gt", gains2.at[pl.ds(0, 15)])

    @pl.when(me != LEAD)
    def _():
        await_sent("gs", gain_src)
        await_all("gt", gain_all)

    gq_out[...] = gain_all[0:1, :]
    gk_out[...] = gain_all[1:2, :]

    for kind, buf, out in (
        ("dv", dv_buf.at[pl.ds(0, 15)], dv_out), ("dk", dk_buf.at[pl.ds(0, 15)], dk_out),
        ("dq0", dq_buf.at[0, pl.ds(0, 15)], dq_out.at[0, pl.ds(0, TC)]),
        ("dq1", dq_buf.at[1, pl.ds(0, 15)], dq_out.at[0, pl.ds(TC, TC)]),
    ):
        await_all(kind, out)
        await_sent(kind, buf)


def hand_over(*refs):
    for i in range(5):
        refs[5 + i][...] = refs[i][...]


def per_device(q, k, v, q_gain, k_gain, noise, codes, exps, step, rewards, gids):
    hbm, vmem = pl.BlockSpec(memory_space=pl.ANY), pl.BlockSpec(memory_space=pltpu.VMEM)
    big = jax.ShapeDtypeStruct((1, TOK, 16 * D), BF16)
    row = jax.ShapeDtypeStruct((1, D), F32)
    dma = pltpu.SemaphoreType.DMA
    halves = (CHUNKS, 16, TC, D)
    results = pl.pallas_call(
        kernel,
        out_shape=(big, big, big, row, row),
        in_specs=[hbm] * 6 + [vmem] * 5,
        out_specs=(hbm, hbm, hbm, vmem, vmem),
        scratch_shapes=[
            pltpu.VMEM((16, TOK, D), BF16),
            pltpu.VMEM((16, TOK, D), BF16),
            pltpu.VMEM(halves, BF16),
            pltpu.VMEM(halves, BF16),
            pltpu.VMEM((16, TOK, D), BF16),
            pltpu.VMEM((TOK, 16 * D), BF16),
            pltpu.VMEM((TOK, 16 * D), jnp.int32),
            pltpu.VMEM((16, TOK), jnp.int32),
            pltpu.VMEM((ROWS, D), BF16),
            pltpu.VMEM((ROWS, D), BF16),
            pltpu.VMEM((D, ROWS), BF16),
            pltpu.VMEM((ROWS, D), BF16),
            pltpu.VMEM((D, ROWS), F32),
            pltpu.VMEM((ROWS, D), BF16),
            pltpu.VMEM((D, ROWS), BF16),
            pltpu.VMEM((ROWS, ROWS), F32),
            pltpu.VMEM((ROWS, ROWS), BF16),
            pltpu.VMEM((ROWS, ROWS), BF16),
            pltpu.VMEM(halves, BF16),
            pltpu.VMEM((16, TOK, D), BF16),
            pltpu.VMEM((16, TOK, D), BF16),
            pltpu.VMEM((1, 128), F32),
            pltpu.VMEM((CHUNKS, GROUPS, 128), F32),
            pltpu.VMEM((CHUNKS, 16, GROUPS, 128), F32),
            pltpu.VMEM((CHUNKS, GROUPS, 128), F32),
            pltpu.VMEM((8, 128), F32),
            pltpu.VMEM((16, 8, 128), F32),
            pltpu.VMEM((8, 128), F32),
            pltpu.VMEM((16, 8, 128), F32),
            pltpu.VMEM((8, 128), F32),
            dma((3,)),
            dma((len(KINDS),)),
            dma((len(KINDS),)),
        ],
        compiler_params=pltpu.CompilerParams(
            collective_id=0, has_side_effects=True, vmem_limit_bytes=58 * 2**20
        ),
    )(
        q.reshape(CHUNKS, TC, 16 * D), k, v, noise, codes, jnp.swapaxes(exps, 1, 2), q_gain.reshape(1, D), k_gain.reshape(1, D),
        step.reshape(1, 1), rewards.reshape(1, 16), gids.reshape(1, 16),
    )
    dq, dk, dv, gq, gk = pl.pallas_call(
        hand_over,
        out_shape=(big, big, big, row, row),
        in_specs=[vmem] * 5,
        out_specs=(vmem,) * 5,
        compiler_params=pltpu.CompilerParams(vmem_limit_bytes=60 * 2**20),
    )(*results)
    return dq, dk, dv, gq.reshape(D), gk.reshape(D)


def solution(mesh):
    tokens = P("dp", "seq", None)
    return jax.shard_map(
        per_device,
        mesh=mesh,
        in_specs=(
            tokens, tokens, tokens, P(), P(), tokens, tokens, tokens, P("dp"), P(), P(),
        ),
        out_specs=(tokens, tokens, tokens, P(), P()),
        check_vma=False,
    )
```

```python
import functools
import math

import jax
import jax.numpy as jnp
from jax import lax
from jax.experimental import pallas as pl
from jax.experimental.pallas import tpu as pltpu
from jax.sharding import PartitionSpec as P

MESH = pl.DeviceIdType.MESH
F32 = jnp.float32
BF16 = jnp.bfloat16
STEPS = 10
EPS = 1e-6
NY, NZ = 2, 8
DZ = (0, 1, 7, 2, 6, 3, 5, 4)
BACK = (0, 2, 1, 4, 3, 6, 5, 7)
TOK, D = 128, 128
ROWS = 2048
CHUNKS = 2
TC = TOK // CHUNKS
RC = ROWS // CHUNKS
TILE = 256
GROUPS = RC // 128
SCALE = 1.0 / math.sqrt(D)
LOG2E = math.log2(math.e)
LEAD = 1

KINDS = ("k", "q", "v", "u0", "u1", "w0", "w1", "dq0", "dq1", "dv", "dk", "gs", "gd", "gt")
ROW = {name: i for i, name in enumerate(KINDS)}


def ring_step(t):
    odd = lax.rem(t, 2)
    return lax.rem(odd * ((t + 1) // 2) + (1 - odd) * (NZ - t // 2), NZ)


def dot(a, b, dims):
    return lax.dot_general(a, b, (dims, ((), ())), preferred_element_type=F32)


def kernel(
    q_in, k_in, v_in, noise_in, codes_in, exps_in, qg_ref, kg_ref, step_ref, rew_ref, gid_ref,
    dq_out, dk_out, dv_out, gq_out, gk_out,
    k_buf, v_buf, q_buf, u_buf, u_src, noise_v, codes_v, exps_v,
    kn, qn, qn_t, attn, d_t, g_nat, g_t, probs, probs_b, ds, dq_buf, dk_buf, dv_buf,
    nsq, part, parts, weights, gain_src, gains, gain_clip, gains2, gain_all,
    load_sem, send_sem, recv_sem,
):
    me = lax.axis_index("seq")
    clip = lax.axis_index("dp")
    y, z = me // NZ, lax.rem(me, NZ)

    def at(m, yy):
        return yy * NZ + lax.rem(z + DZ[m], NZ)

    def others():
        yield (1 - y) * NZ + z, y
        for m in range(1, NZ):
            for yy in range(NY):
                yield at(m, yy), 2 * BACK[m] + y

    def remote(kind, src, dst, peer, axis="seq"):
        return pltpu.make_async_remote_copy(
            src_ref=src, dst_ref=dst, send_sem=send_sem.at[ROW[kind]], recv_sem=recv_sem.at[ROW[kind]],
            device_id={axis: peer}, device_id_type=MESH,
        )

    def send(kind, src, dst, peer, axis="seq"):
        remote(kind, src, dst, peer, axis).start()

    def own(kind, src, dst):
        pltpu.make_async_copy(src, dst, recv_sem.at[ROW[kind]]).start()

    def await_all(kind, ref):
        remote(kind, ref, ref, me).wait_recv()

    def await_sent(kind, ref):
        remote(kind, ref, ref, me).wait_send()

    loads = [
        pltpu.make_async_copy(noise_in.at[0], noise_v, load_sem.at[0]),
        pltpu.make_async_copy(codes_in.at[0], codes_v, load_sem.at[1]),
        pltpu.make_async_copy(exps_in.at[0], exps_v, load_sem.at[2]),
    ]
    for c in loads:
        c.start()

    barrier = pltpu.get_barrier_semaphore()
    for peer, _ in others():
        pl.semaphore_signal(barrier, inc=1, device_id={"seq": peer}, device_id_type=MESH)

    @pl.when(me == LEAD)
    def _():
        for j in range(1, 16):
            pl.semaphore_signal(
                barrier, inc=1, device_id={"dp": lax.rem(clip + j, 16)}, device_id_type=MESH
            )
        pl.semaphore_wait(barrier, 30)

    @pl.when(me != LEAD)
    def _():
        pl.semaphore_wait(barrier, 15)

    def cols(ref, head):
        return ref.at[0, :, pl.ds(pl.multiple_of(head * D, D), D)]

    def halves_of(ref, head):
        return ref.at[:, :, pl.ds(pl.multiple_of(head * D, D), D)]

    for peer, there in others():
        send("k", cols(k_in, peer), k_buf.at[there], peer)
    own("k", cols(k_in, me), k_buf.at[y])
    for peer, there in others():
        send("q", halves_of(q_in, peer), q_buf.at[:, there], peer)
    own("q", halves_of(q_in, me), q_buf.at[:, y])
    for peer, there in others():
        send("v", cols(v_in, peer), v_buf.at[there], peer)
    own("v", cols(v_in, me), v_buf.at[y])

    level = 1.0 - jnp.broadcast_to(step_ref[...].astype(F32), (1, 128)) / STEPS
    step_size = 1.0 / STEPS
    ratio = step_size / (0.7 * jnp.sqrt(step_size * level / (1.0 - level)))
    gid = gid_ref[...].astype(F32)
    rewards = rew_ref[...]
    picked = (lax.broadcasted_iota(jnp.int32, gid.shape, 1) == clip).astype(F32)
    own_gid = jnp.sum(picked * gid, axis=1, keepdims=True)
    same = (gid == own_gid).astype(F32)
    advantage = jnp.sum(picked * rewards, axis=1, keepdims=True) - jnp.sum(
        same * rewards, axis=1, keepdims=True
    ) / jnp.sum(same, axis=1, keepdims=True)

    for c in loads:
        c.wait()
    scales = jnp.transpose(jnp.exp2(exps_v[...].astype(F32)))
    noise_sq = jnp.zeros((TOK, D), F32)
    for h in range(16):
        code = codes_v[:, h * D:(h + 1) * D]
        magnitude = ((8 + (code & 7)) << ((code >> 3) & 15)).astype(F32) * (1.0 / 1024.0)
        old = jnp.where(code >= 128, -magnitude, magnitude) * scales[:, h:h + 1]
        noise = noise_v[:, h * D:(h + 1) * D].astype(F32)
        u_src[h] = (noise - ratio * old.astype(BF16).astype(F32)).astype(BF16)
        noise_sq = noise_sq + noise * noise
    nsq[...] = jnp.sum(jnp.transpose(noise_sq), axis=0, keepdims=True)

    def send_u(c):
        rows = pl.ds(c * TC, TC)
        for peer, there in others():
            send("u%d" % c, u_src.at[peer, rows], u_buf.at[c, there], peer)
        own("u%d" % c, u_src.at[me, rows], u_buf.at[c, y])

    send_u(0)
    send_u(1)

    def normed(x, gain):
        rinv = lax.rsqrt(jnp.mean(x * x, axis=1, keepdims=True) + EPS)
        return (gain * x * rinv).astype(BF16)

    await_all("k", k_buf)

    @pl.loop(0, 16)
    def _(n):
        kn[pl.ds(pl.multiple_of(n * D, D), D), :] = normed(k_buf[n].astype(F32), kg_ref[...])

    await_all("q", q_buf)

    def block(ref, g):
        c, m = g // GROUPS, lax.rem(g, GROUPS)
        return ref[c, pl.ds(m * CHUNKS, CHUNKS)].reshape(128, D)

    def rows_of(g, size=128):
        return pl.ds(pl.multiple_of(g * size, size), size)

    @pl.loop(0, 16)
    def _(g):
        x = normed(block(q_buf, g).astype(F32), qg_ref[...])
        qn[rows_of(g), :] = x
        qn_t[:, rows_of(g)] = jnp.transpose(x.astype(F32)).astype(BF16)

    @pl.loop(0, ROWS // TILE)
    def _(i):
        rows = rows_of(i, TILE)
        s = dot(qn[rows, :], kn[...], ((1,), (1,)))
        e = jnp.exp2((s - jnp.max(s, axis=1, keepdims=True)) * (SCALE * LOG2E))
        p = e * (1.0 / jnp.sum(e, axis=1, keepdims=True))
        probs[rows, :] = p
        probs_b[rows, :] = p.astype(BF16)

    await_all("v", v_buf)

    def values():
        return v_buf[...].reshape(ROWS, D)

    @pl.loop(0, ROWS // TILE)
    def _(i):
        rows = rows_of(i, TILE)
        attn[rows, :] = dot(probs_b[rows, :], values(), ((1,), (0,))).astype(BF16)

    for c in range(CHUNKS):
        await_all("u%d" % c, u_buf.at[c])

        @pl.loop(0, GROUPS)
        def _(m, c=c):
            g = c * GROUPS + m
            rows = rows_of(g)
            x = block(u_buf, g).astype(F32) + ratio * attn[rows, :].astype(F32)
            x_t = jnp.transpose(x)
            d_t[:, rows] = x_t
            part[c, pl.ds(lax.rem(z + ring_step(m), NZ), 1), :] = jnp.sum(
                x_t * x_t, axis=0, keepdims=True
            )

        line = nsq[...]
        halves = jnp.where(y == c, line, jnp.concatenate([line[:, TC:], line[:, :TC]], axis=1))
        shape = (GROUPS, 128)
        here = (lax.broadcasted_iota(jnp.int32, shape, 0) == z) & (
            lax.broadcasted_iota(jnp.int32, shape, 1) // TC == y
        )
        mine = part[c] - jnp.where(here, jnp.broadcast_to(halves, shape), 0.0)
        part[c] = mine
        parts[c, me] = mine
        for peer, _ in others():
            send("w%d" % c, part.at[c], parts.at[c, me], peer)

    def weigh(c):
        await_all("w%d" % c, parts.at[c, pl.ds(0, 15)])
        total = jnp.sum(parts[c], axis=0)
        weights[c] = advantage * jnp.exp(total * (-1.0 / (2.0 * ROWS))) * ratio

    def weigh_block(g):
        c, m = g // GROUPS, lax.rem(g, GROUPS)
        rows = rows_of(g)
        w = weights[c, pl.ds(lax.rem(z + ring_step(m), NZ), 1), :]
        x = w * d_t[:, rows]
        g_t[:, rows] = x.astype(BF16)
        g_nat[rows, :] = jnp.transpose(x).astype(BF16)

    def out_copy(kind, src, dst, peer):
        @pl.when(peer != me)
        def _():
            send(kind, src, dst, peer)

        @pl.when(peer == me)
        def _():
            own(kind, src, dst)

    def own_cols(ref):
        return ref.at[0, :, pl.ds(pl.multiple_of(me * D, D), D)]

    def own_piece(ref, c):
        return ref.at[0, pl.ds(c * TC, TC), pl.ds(pl.multiple_of(me * D, D), D)]

    def norm_back(x, gain, grad):
        rinv = lax.rsqrt(jnp.mean(x * x, axis=1, keepdims=True) + EPS)
        scaled = gain * grad
        inner = jnp.sum(scaled * x, axis=1, keepdims=True)
        out = rinv * scaled - x * (rinv * rinv * rinv * inner * (1.0 / D))
        return out.astype(BF16), jnp.sum(grad * x * rinv, axis=0, keepdims=True)

    def dscore_rows(i):
        rows = rows_of(i, TILE)
        g = g_nat[rows, :]
        delta = jnp.sum(g.astype(F32) * attn[rows, :].astype(F32), axis=1, keepdims=True)
        dp = dot(g, values(), ((1,), (1,)))
        ds[rows, :] = (probs[rows, :] * (dp - delta)).astype(BF16)

    per_tile = TILE // TC

    def query_rows(c, i):
        rows = rows_of(c * (RC // TILE) + i, TILE)
        grad = dot(ds[rows, :], kn[...], ((1,), (0,))) * SCALE
        x = q_buf[c, pl.ds(i * per_tile, per_tile)].reshape(TILE, D).astype(F32)
        out, gain = norm_back(x, qg_ref[...], grad)
        dq_buf[c, pl.ds(i * per_tile, per_tile)] = out.reshape(per_tile, TC, D)
        gain_src[0:1, :] = gain_src[0:1, :] + gain

    def send_query_rows(c, i):
        for j in range(per_tile):
            slot = i * per_tile + j
            peer = (j % NY) * NZ + lax.rem(z + ring_step(slot // 2), NZ)
            out_copy("dq%d" % c, dq_buf.at[c, slot], own_piece(dq_out, c), peer)

    gain_src[...] = jnp.zeros_like(gain_src)

    weigh(0)

    @pl.loop(0, RC // TILE)
    def _(i):
        for j in range(TILE // 128):
            weigh_block(i * (TILE // 128) + j)
        dscore_rows(i)
        query_rows(0, i)
        send_query_rows(0, i)

    weigh(1)

    @pl.loop(GROUPS, 2 * GROUPS)
    def _(g):
        weigh_block(g)

    @pl.loop(0, NZ)
    def _(t):
        wide = rows_of(t, 256)
        acc = dot(g_t[...], probs_b[:, wide], ((1,), (0,)))
        for j in range(NY):
            slot = t * NY + j
            dv_buf[slot] = jnp.transpose(acc[:, j * D:(j + 1) * D]).astype(BF16)
            peer = j * NZ + lax.rem(z + ring_step(t), NZ)
            out_copy("dv", dv_buf.at[slot], own_cols(dv_out), peer)

    @pl.loop(0, RC // TILE)
    def _(i):
        dscore_rows(RC // TILE + i)
        query_rows(1, i)

    @pl.loop(0, NZ)
    def _(t):
        wide = rows_of(t, 256)
        acc = dot(qn_t[...], ds[:, wide], ((1,), (0,)))
        for j in range(NY):
            slot = t * NY + j
            grad = jnp.transpose(acc[:, j * D:(j + 1) * D]) * SCALE
            out, gain = norm_back(k_buf[slot].astype(F32), kg_ref[...], grad)
            dk_buf[slot] = out
            gain_src[1:2, :] = gain_src[1:2, :] + gain

    @pl.when(me != LEAD)
    def _():
        send("gs", gain_src, gains.at[me], LEAD)

    @pl.when(me == LEAD)
    def _():
        gains[me] = gain_src[...]

    def send_keys(first, last):
        @pl.loop(first, last)
        def _(t):
            for j in range(NY):
                slot = t * NY + j
                peer = j * NZ + lax.rem(z + ring_step(t), NZ)
                out_copy("dk", dk_buf.at[slot], own_cols(dk_out), peer)

    send_keys(0, NZ // 2)

    @pl.when(me == LEAD)
    def _():
        await_all("gs", gains.at[pl.ds(0, 15)])
        total = jnp.sum(gains[...], axis=0)
        gain_clip[...] = total
        gains2[clip] = total
        for j in range(1, 16):
            send("gd", gain_clip, gains2.at[clip], lax.rem(clip + j, 16), "dp")

    send_keys(NZ // 2, NZ)

    @pl.loop(0, RC // TILE - 1)
    def _(i):
        send_query_rows(1, i)

    @pl.when(me == LEAD)
    def _():
        await_all("gd", gains2.at[pl.ds(0, 15)])
        gain_all[...] = jnp.sum(gains2[...], axis=0) * (1.0 / math.sqrt(16.0 * 16.0 * ROWS))
        for peer, _ in others():
            send("gt", gain_all, gain_all, peer)

    send_query_rows(1, RC // TILE - 1)

    for kind, ref in (
        ("k", k_buf.at[pl.ds(0, 15)]), ("q", q_buf.at[:, pl.ds(0, 15)]), ("v", v_buf.at[pl.ds(0, 15)]),
        ("u0", u_buf.at[0, pl.ds(0, 15)]), ("u1", u_buf.at[1, pl.ds(0, 15)]),
        ("w0", parts.at[0, pl.ds(0, 15)]), ("w1", parts.at[1, pl.ds(0, 15)]),
    ):
        await_sent(kind, ref)

    @pl.when(me == LEAD)
    def _():
        await_sent("gd", gains2.at[pl.ds(0, 15)])
        await_sent("gt", gains2.at[pl.ds(0, 15)])

    @pl.when(me != LEAD)
    def _():
        await_sent("gs", gain_src)
        await_all("gt", gain_all)

    gq_out[...] = gain_all[0:1, :]
    gk_out[...] = gain_all[1:2, :]

    for kind, buf, out in (
        ("dv", dv_buf.at[pl.ds(0, 15)], dv_out), ("dk", dk_buf.at[pl.ds(0, 15)], dk_out),
        ("dq0", dq_buf.at[0, pl.ds(0, 15)], dq_out.at[0, pl.ds(0, TC)]),
        ("dq1", dq_buf.at[1, pl.ds(0, 15)], dq_out.at[0, pl.ds(TC, TC)]),
    ):
        await_all(kind, out)
        await_sent(kind, buf)


def hand_over(*refs):
    n = (len(refs) - 1) // 2
    copies = [pltpu.make_async_copy(refs[i], refs[n + i], refs[-1].at[i]) for i in range(n)]
    for c in copies:
        c.start()
    for c in copies:
        c.wait()


def per_device(q, k, v, q_gain, k_gain, noise, codes, exps, step, rewards, gids):
    hbm, vmem = pl.BlockSpec(memory_space=pl.ANY), pl.BlockSpec(memory_space=pltpu.VMEM)
    big = jax.ShapeDtypeStruct((1, TOK, 16 * D), BF16)
    row = jax.ShapeDtypeStruct((1, D), F32)
    dma = pltpu.SemaphoreType.DMA
    halves = (CHUNKS, 16, TC, D)
    results = pl.pallas_call(
        kernel,
        out_shape=(pltpu.VMEM((1, TOK, 16 * D), BF16),) * 3 + (pltpu.VMEM((1, D), F32),) * 2,
        in_specs=[pl.BlockSpec(memory_space=pltpu.HBM)] * 6 + [vmem] * 5,
        out_specs=(vmem,) * 5,
        scratch_shapes=[
            pltpu.VMEM((16, TOK, D), BF16),
            pltpu.VMEM((16, TOK, D), BF16),
            pltpu.VMEM(halves, BF16),
            pltpu.VMEM(halves, BF16),
            pltpu.VMEM((16, TOK, D), BF16),
            pltpu.VMEM((TOK, 16 * D), BF16),
            pltpu.VMEM((TOK, 16 * D), jnp.int32),
            pltpu.VMEM((16, TOK), jnp.int32),
            pltpu.VMEM((ROWS, D), BF16),
            pltpu.VMEM((ROWS, D), BF16),
            pltpu.VMEM((D, ROWS), BF16),
            pltpu.VMEM((ROWS, D), BF16),
            pltpu.VMEM((D, ROWS), F32),
            pltpu.VMEM((ROWS, D), BF16),
            pltpu.VMEM((D, ROWS), BF16),
            pltpu.VMEM((ROWS, ROWS), F32),
            pltpu.VMEM((ROWS, ROWS), BF16),
            pltpu.VMEM((ROWS, ROWS), BF16),
            pltpu.VMEM(halves, BF16),
            pltpu.VMEM((16, TOK, D), BF16),
            pltpu.VMEM((16, TOK, D), BF16),
            pltpu.VMEM((1, 128), F32),
            pltpu.VMEM((CHUNKS, GROUPS, 128), F32),
            pltpu.VMEM((CHUNKS, 16, GROUPS, 128), F32),
            pltpu.VMEM((CHUNKS, GROUPS, 128), F32),
            pltpu.VMEM((8, 128), F32),
            pltpu.VMEM((16, 8, 128), F32),
            pltpu.VMEM((8, 128), F32),
            pltpu.VMEM((16, 8, 128), F32),
            pltpu.VMEM((8, 128), F32),
            dma((3,)),
            dma((len(KINDS),)),
            dma((len(KINDS),)),
        ],
        compiler_params=pltpu.CompilerParams(
            collective_id=0, has_side_effects=True, vmem_limit_bytes=56 * 2**20
        ),
    )(
        q.reshape(CHUNKS, TC, 16 * D), k, v, noise, codes, jnp.swapaxes(exps, 1, 2), q_gain.reshape(1, D), k_gain.reshape(1, D),
        step.reshape(1, 1), rewards.reshape(1, 16), gids.reshape(1, 16),
    )
    dq, dk, dv, gq, gk = pl.pallas_call(
        hand_over,
        out_shape=(big, big, big, row, row),
        in_specs=[vmem] * 5,
        out_specs=(pl.BlockSpec(memory_space=pltpu.HBM),) * 5,
        scratch_shapes=[dma((5,))],
        compiler_params=pltpu.CompilerParams(vmem_limit_bytes=60 * 2**20),
    )(*[pltpu.with_memory_space_constraint(r, pltpu.VMEM) for r in results])
    return dq, dk, dv, gq.reshape(D), gk.reshape(D)


def solution(mesh):
    tokens = P("dp", "seq", None)
    return jax.shard_map(
        per_device,
        mesh=mesh,
        in_specs=(
            tokens, tokens, tokens, P(), P(), tokens, tokens, tokens, P("dp"), P(), P(),
        ),
        out_specs=(tokens, tokens, tokens, P(), P()),
        check_vma=False,
    )
```

```python
import functools
import math

import jax
import jax.numpy as jnp
from jax import lax
from jax.experimental import pallas as pl
from jax.experimental.pallas import tpu as pltpu
from jax.sharding import PartitionSpec as P

MESH = pl.DeviceIdType.MESH
F32 = jnp.float32
BF16 = jnp.bfloat16
STEPS = 10
EPS = 1e-6
NY, NZ = 2, 8
DZ = (4, 5, 3, 6, 2, 7, 1, 0)
BACK = (0, 2, 1, 4, 3, 6, 5, 7)
TOK, D = 128, 128
ROWS = 2048
CHUNKS = 2
TC = TOK // CHUNKS
RC = ROWS // CHUNKS
TILE = 256
GROUPS = RC // 128
SCALE = 1.0 / math.sqrt(D)
LOG2E = math.log2(math.e)
LEAD = 1

KINDS = ("k", "q", "v", "u0", "u1", "w0", "w1", "dq0", "dq1", "dv", "dk", "gs", "gd", "gt")
ROW = {name: i for i, name in enumerate(KINDS)}


def ring_step(t):
    odd = lax.rem(t, 2)
    half = NZ // 2
    return lax.rem(odd * (half + (t + 1) // 2) + (1 - odd) * (half - t // 2), NZ)


def dot(a, b, dims):
    return lax.dot_general(a, b, (dims, ((), ())), preferred_element_type=F32)


def kernel(
    q_in, k_in, v_in, noise_in, codes_in, exps_in, qg_ref, kg_ref, step_ref, rew_ref, gid_ref,
    dq_out, dk_out, dv_out, gq_out, gk_out,
    k_buf, v_buf, q_buf, u_buf, u_src, noise_v, codes_v, exps_v,
    kn, qn, qn_t, attn, d_t, g_nat, g_t, probs, probs_b, ds, dq_buf, dk_buf, dv_buf,
    nsq, part, parts, weights, gain_src, gains, gain_clip, gains2, gain_all,
    load_sem, send_sem, recv_sem,
):
    me = lax.axis_index("seq")
    clip = lax.axis_index("dp")
    y, z = me // NZ, lax.rem(me, NZ)
    home = 2 * (NZ - 1) + y

    def at(m, yy):
        return yy * NZ + lax.rem(z + DZ[m], NZ)

    def others():
        for m in range(NZ - 1):
            for yy in range(NY):
                yield at(m, yy), 2 * BACK[m] + y
        yield (1 - y) * NZ + z, home

    def remote(kind, src, dst, peer, axis="seq"):
        return pltpu.make_async_remote_copy(
            src_ref=src, dst_ref=dst, send_sem=send_sem.at[ROW[kind]], recv_sem=recv_sem.at[ROW[kind]],
            device_id={axis: peer}, device_id_type=MESH,
        )

    def send(kind, src, dst, peer, axis="seq"):
        remote(kind, src, dst, peer, axis).start()

    def own(kind, src, dst):
        pltpu.make_async_copy(src, dst, recv_sem.at[ROW[kind]]).start()

    def await_all(kind, ref):
        remote(kind, ref, ref, me).wait_recv()

    def await_sent(kind, ref):
        remote(kind, ref, ref, me).wait_send()

    loads = [
        pltpu.make_async_copy(noise_in.at[0], noise_v, load_sem.at[0]),
        pltpu.make_async_copy(codes_in.at[0], codes_v, load_sem.at[1]),
        pltpu.make_async_copy(exps_in.at[0], exps_v, load_sem.at[2]),
    ]
    for c in loads:
        c.start()

    barrier = pltpu.get_barrier_semaphore()
    for peer, _ in others():
        pl.semaphore_signal(barrier, inc=1, device_id={"seq": peer}, device_id_type=MESH)

    @pl.when(me == LEAD)
    def _():
        for j in range(1, 16):
            pl.semaphore_signal(
                barrier, inc=1, device_id={"dp": lax.rem(clip + j, 16)}, device_id_type=MESH
            )
        pl.semaphore_wait(barrier, 30)

    @pl.when(me != LEAD)
    def _():
        pl.semaphore_wait(barrier, 15)

    def cols(ref, head):
        return ref.at[0, :, pl.ds(pl.multiple_of(head * D, D), D)]

    def halves_of(ref, head):
        return ref.at[:, :, pl.ds(pl.multiple_of(head * D, D), D)]

    for peer, there in others():
        send("k", cols(k_in, peer), k_buf.at[there], peer)
    own("k", cols(k_in, me), k_buf.at[home])
    for peer, there in others():
        send("q", halves_of(q_in, peer), q_buf.at[:, there], peer)
    own("q", halves_of(q_in, me), q_buf.at[:, home])
    for peer, there in others():
        send("v", cols(v_in, peer), v_buf.at[there], peer)
    own("v", cols(v_in, me), v_buf.at[home])

    level = 1.0 - jnp.broadcast_to(step_ref[...].astype(F32), (1, 128)) / STEPS
    step_size = 1.0 / STEPS
    ratio = step_size / (0.7 * jnp.sqrt(step_size * level / (1.0 - level)))
    gid = gid_ref[...].astype(F32)
    rewards = rew_ref[...]
    picked = (lax.broadcasted_iota(jnp.int32, gid.shape, 1) == clip).astype(F32)
    own_gid = jnp.sum(picked * gid, axis=1, keepdims=True)
    same = (gid == own_gid).astype(F32)
    advantage = jnp.sum(picked * rewards, axis=1, keepdims=True) - jnp.sum(
        same * rewards, axis=1, keepdims=True
    ) / jnp.sum(same, axis=1, keepdims=True)

    for c in loads:
        c.wait()
    scales = jnp.transpose(jnp.exp2(exps_v[...].astype(F32)))
    noise_sq = jnp.zeros((TOK, D), F32)
    for h in range(16):
        code = codes_v[:, h * D:(h + 1) * D]
        magnitude = ((8 + (code & 7)) << ((code >> 3) & 15)).astype(F32) * (1.0 / 1024.0)
        old = jnp.where(code >= 128, -magnitude, magnitude) * scales[:, h:h + 1]
        noise = noise_v[:, h * D:(h + 1) * D].astype(F32)
        u_src[h] = (noise - ratio * old.astype(BF16).astype(F32)).astype(BF16)
        noise_sq = noise_sq + noise * noise
    nsq[...] = jnp.sum(jnp.transpose(noise_sq), axis=0, keepdims=True)

    def send_u(c):
        rows = pl.ds(c * TC, TC)
        for peer, there in others():
            send("u%d" % c, u_src.at[peer, rows], u_buf.at[c, there], peer)
        own("u%d" % c, u_src.at[me, rows], u_buf.at[c, home])

    send_u(0)
    send_u(1)

    def normed(x, gain):
        rinv = lax.rsqrt(jnp.mean(x * x, axis=1, keepdims=True) + EPS)
        return (gain * x * rinv).astype(BF16)

    await_all("k", k_buf)

    @pl.loop(0, 16)
    def _(n):
        kn[pl.ds(pl.multiple_of(n * D, D), D), :] = normed(k_buf[n].astype(F32), kg_ref[...])

    await_all("q", q_buf)

    def block(ref, g):
        c, m = g // GROUPS, lax.rem(g, GROUPS)
        return ref[c, pl.ds(m * CHUNKS, CHUNKS)].reshape(128, D)

    def rows_of(g, size=128):
        return pl.ds(pl.multiple_of(g * size, size), size)

    @pl.loop(0, 16)
    def _(g):
        x = normed(block(q_buf, g).astype(F32), qg_ref[...])
        qn[rows_of(g), :] = x
        qn_t[:, rows_of(g)] = jnp.transpose(x.astype(F32)).astype(BF16)

    @pl.loop(0, ROWS // TILE)
    def _(i):
        rows = rows_of(i, TILE)
        s = dot(qn[rows, :], kn[...], ((1,), (1,)))
        e = jnp.exp2((s - jnp.max(s, axis=1, keepdims=True)) * (SCALE * LOG2E))
        p = e * (1.0 / jnp.sum(e, axis=1, keepdims=True))
        probs[rows, :] = p
        probs_b[rows, :] = p.astype(BF16)

    await_all("v", v_buf)

    def values():
        return v_buf[...].reshape(ROWS, D)

    @pl.loop(0, ROWS // TILE)
    def _(i):
        rows = rows_of(i, TILE)
        attn[rows, :] = dot(probs_b[rows, :], values(), ((1,), (0,))).astype(BF16)

    for c in range(CHUNKS):
        await_all("u%d" % c, u_buf.at[c])

        @pl.loop(0, GROUPS)
        def _(m, c=c):
            g = c * GROUPS + m
            rows = rows_of(g)
            x = block(u_buf, g).astype(F32) + ratio * attn[rows, :].astype(F32)
            x_t = jnp.transpose(x)
            d_t[:, rows] = x_t
            part[c, pl.ds(lax.rem(z + ring_step(m), NZ), 1), :] = jnp.sum(
                x_t * x_t, axis=0, keepdims=True
            )

        line = nsq[...]
        halves = jnp.where(y == c, line, jnp.concatenate([line[:, TC:], line[:, :TC]], axis=1))
        shape = (GROUPS, 128)
        here = (lax.broadcasted_iota(jnp.int32, shape, 0) == z) & (
            lax.broadcasted_iota(jnp.int32, shape, 1) // TC == y
        )
        mine = part[c] - jnp.where(here, jnp.broadcast_to(halves, shape), 0.0)
        part[c] = mine
        parts[c, me] = mine
        for peer, _ in others():
            send("w%d" % c, part.at[c], parts.at[c, me], peer)

    def weigh(c):
        await_all("w%d" % c, parts.at[c, pl.ds(0, 15)])
        total = jnp.sum(parts[c], axis=0)
        weights[c] = advantage * jnp.exp(total * (-1.0 / (2.0 * ROWS))) * ratio

    def weigh_block(g):
        c, m = g // GROUPS, lax.rem(g, GROUPS)
        rows = rows_of(g)
        w = weights[c, pl.ds(lax.rem(z + ring_step(m), NZ), 1), :]
        x = w * d_t[:, rows]
        g_t[:, rows] = x.astype(BF16)
        g_nat[rows, :] = jnp.transpose(x).astype(BF16)

    def out_copy(kind, src, dst, peer):
        @pl.when(peer != me)
        def _():
            send(kind, src, dst, peer)

        @pl.when(peer == me)
        def _():
            own(kind, src, dst)

    def own_cols(ref):
        return ref.at[0, :, pl.ds(pl.multiple_of(me * D, D), D)]

    def own_piece(ref, c):
        return ref.at[0, pl.ds(c * TC, TC), pl.ds(pl.multiple_of(me * D, D), D)]

    def norm_back(x, gain, grad):
        rinv = lax.rsqrt(jnp.mean(x * x, axis=1, keepdims=True) + EPS)
        scaled = gain * grad
        inner = jnp.sum(scaled * x, axis=1, keepdims=True)
        out = rinv * scaled - x * (rinv * rinv * rinv * inner * (1.0 / D))
        return out.astype(BF16), jnp.sum(grad * x * rinv, axis=0, keepdims=True)

    def dscore_rows(i):
        rows = rows_of(i, TILE)
        g = g_nat[rows, :]
        delta = jnp.sum(g.astype(F32) * attn[rows, :].astype(F32), axis=1, keepdims=True)
        dp = dot(g, values(), ((1,), (1,)))
        ds[rows, :] = (probs[rows, :] * (dp - delta)).astype(BF16)

    per_tile = TILE // TC

    def query_rows(c, i):
        rows = rows_of(c * (RC // TILE) + i, TILE)
        grad = dot(ds[rows, :], kn[...], ((1,), (0,))) * SCALE
        x = q_buf[c, pl.ds(i * per_tile, per_tile)].reshape(TILE, D).astype(F32)
        out, gain = norm_back(x, qg_ref[...], grad)
        dq_buf[c, pl.ds(i * per_tile, per_tile)] = out.reshape(per_tile, TC, D)
        gain_src[0:1, :] = gain_src[0:1, :] + gain

    def send_query_rows(c, i):
        for j in range(per_tile):
            slot = i * per_tile + j
            peer = (j % NY) * NZ + lax.rem(z + ring_step(slot // 2), NZ)
            out_copy("dq%d" % c, dq_buf.at[c, slot], own_piece(dq_out, c), peer)

    gain_src[...] = jnp.zeros_like(gain_src)

    weigh(0)

    @pl.loop(0, RC // TILE)
    def _(i):
        for j in range(TILE // 128):
            weigh_block(i * (TILE // 128) + j)
        dscore_rows(i)
        query_rows(0, i)
        send_query_rows(0, i)

    weigh(1)

    @pl.loop(GROUPS, 2 * GROUPS)
    def _(g):
        weigh_block(g)

    @pl.loop(0, NZ)
    def _(t):
        wide = rows_of(t, 256)
        acc = dot(g_t[...], probs_b[:, wide], ((1,), (0,)))
        for j in range(NY):
            slot = t * NY + j
            dv_buf[slot] = jnp.transpose(acc[:, j * D:(j + 1) * D]).astype(BF16)
            peer = j * NZ + lax.rem(z + ring_step(t), NZ)
            out_copy("dv", dv_buf.at[slot], own_cols(dv_out), peer)

    @pl.loop(0, RC // TILE)
    def _(i):
        dscore_rows(RC // TILE + i)
        query_rows(1, i)

    @pl.loop(0, NZ)
    def _(t):
        wide = rows_of(t, 256)
        acc = dot(qn_t[...], ds[:, wide], ((1,), (0,)))
        for j in range(NY):
            slot = t * NY + j
            grad = jnp.transpose(acc[:, j * D:(j + 1) * D]) * SCALE
            out, gain = norm_back(k_buf[slot].astype(F32), kg_ref[...], grad)
            dk_buf[slot] = out
            gain_src[1:2, :] = gain_src[1:2, :] + gain

    @pl.when(me != LEAD)
    def _():
        send("gs", gain_src, gains.at[me], LEAD)

    @pl.when(me == LEAD)
    def _():
        gains[me] = gain_src[...]

    def send_keys(first, last):
        @pl.loop(first, last)
        def _(t):
            for j in range(NY):
                slot = t * NY + j
                peer = j * NZ + lax.rem(z + ring_step(t), NZ)
                out_copy("dk", dk_buf.at[slot], own_cols(dk_out), peer)

    send_keys(0, NZ // 2)

    @pl.when(me == LEAD)
    def _():
        await_all("gs", gains.at[pl.ds(0, 15)])
        total = jnp.sum(gains[...], axis=0)
        gain_clip[...] = total
        gains2[clip] = total
        for j in range(1, 16):
            send("gd", gain_clip, gains2.at[clip], lax.rem(clip + j, 16), "dp")

    send_keys(NZ // 2, NZ)

    @pl.loop(0, RC // TILE - 1)
    def _(i):
        send_query_rows(1, i)

    @pl.when(me == LEAD)
    def _():
        await_all("gd", gains2.at[pl.ds(0, 15)])
        gain_all[...] = jnp.sum(gains2[...], axis=0) * (1.0 / math.sqrt(16.0 * 16.0 * ROWS))
        for peer, _ in others():
            send("gt", gain_all, gain_all, peer)

    send_query_rows(1, RC // TILE - 1)

    for kind, ref in (
        ("k", k_buf.at[pl.ds(0, 15)]), ("q", q_buf.at[:, pl.ds(0, 15)]), ("v", v_buf.at[pl.ds(0, 15)]),
        ("u0", u_buf.at[0, pl.ds(0, 15)]), ("u1", u_buf.at[1, pl.ds(0, 15)]),
        ("w0", parts.at[0, pl.ds(0, 15)]), ("w1", parts.at[1, pl.ds(0, 15)]),
    ):
        await_sent(kind, ref)

    @pl.when(me == LEAD)
    def _():
        await_sent("gd", gains2.at[pl.ds(0, 15)])
        await_sent("gt", gains2.at[pl.ds(0, 15)])

    @pl.when(me != LEAD)
    def _():
        await_sent("gs", gain_src)
        await_all("gt", gain_all)

    gq_out[...] = gain_all[0:1, :]
    gk_out[...] = gain_all[1:2, :]

    for kind, buf, out in (
        ("dv", dv_buf.at[pl.ds(0, 15)], dv_out), ("dk", dk_buf.at[pl.ds(0, 15)], dk_out),
        ("dq0", dq_buf.at[0, pl.ds(0, 15)], dq_out.at[0, pl.ds(0, TC)]),
        ("dq1", dq_buf.at[1, pl.ds(0, 15)], dq_out.at[0, pl.ds(TC, TC)]),
    ):
        await_all(kind, out)
        await_sent(kind, buf)


def hand_over(*refs):
    n = (len(refs) - 1) // 2
    copies = [pltpu.make_async_copy(refs[i], refs[n + i], refs[-1].at[i]) for i in range(n)]
    for c in copies:
        c.start()
    for c in copies:
        c.wait()


def per_device(q, k, v, q_gain, k_gain, noise, codes, exps, step, rewards, gids):
    hbm, vmem = pl.BlockSpec(memory_space=pl.ANY), pl.BlockSpec(memory_space=pltpu.VMEM)
    big = jax.ShapeDtypeStruct((1, TOK, 16 * D), BF16)
    row = jax.ShapeDtypeStruct((1, D), F32)
    dma = pltpu.SemaphoreType.DMA
    halves = (CHUNKS, 16, TC, D)
    results = pl.pallas_call(
        kernel,
        out_shape=(pltpu.VMEM((1, TOK, 16 * D), BF16),) * 3 + (pltpu.VMEM((1, D), F32),) * 2,
        in_specs=[pl.BlockSpec(memory_space=pltpu.HBM)] * 6 + [vmem] * 5,
        out_specs=(vmem,) * 5,
        scratch_shapes=[
            pltpu.VMEM((16, TOK, D), BF16),
            pltpu.VMEM((16, TOK, D), BF16),
            pltpu.VMEM(halves, BF16),
            pltpu.VMEM(halves, BF16),
            pltpu.VMEM((16, TOK, D), BF16),
            pltpu.VMEM((TOK, 16 * D), BF16),
            pltpu.VMEM((TOK, 16 * D), jnp.int32),
            pltpu.VMEM((16, TOK), jnp.int32),
            pltpu.VMEM((ROWS, D), BF16),
            pltpu.VMEM((ROWS, D), BF16),
            pltpu.VMEM((D, ROWS), BF16),
            pltpu.VMEM((ROWS, D), BF16),
            pltpu.VMEM((D, ROWS), F32),
            pltpu.VMEM((ROWS, D), BF16),
            pltpu.VMEM((D, ROWS), BF16),
            pltpu.VMEM((ROWS, ROWS), F32),
            pltpu.VMEM((ROWS, ROWS), BF16),
            pltpu.VMEM((ROWS, ROWS), BF16),
            pltpu.VMEM(halves, BF16),
            pltpu.VMEM((16, TOK, D), BF16),
            pltpu.VMEM((16, TOK, D), BF16),
            pltpu.VMEM((1, 128), F32),
            pltpu.VMEM((CHUNKS, GROUPS, 128), F32),
            pltpu.VMEM((CHUNKS, 16, GROUPS, 128), F32),
            pltpu.VMEM((CHUNKS, GROUPS, 128), F32),
            pltpu.VMEM((8, 128), F32),
            pltpu.VMEM((16, 8, 128), F32),
            pltpu.VMEM((8, 128), F32),
            pltpu.VMEM((16, 8, 128), F32),
            pltpu.VMEM((8, 128), F32),
            dma((3,)),
            dma((len(KINDS),)),
            dma((len(KINDS),)),
        ],
        compiler_params=pltpu.CompilerParams(
            collective_id=0, has_side_effects=True, vmem_limit_bytes=56 * 2**20
        ),
    )(
        q.reshape(CHUNKS, TC, 16 * D), k, v, noise, codes, jnp.swapaxes(exps, 1, 2), q_gain.reshape(1, D), k_gain.reshape(1, D),
        step.reshape(1, 1), rewards.reshape(1, 16), gids.reshape(1, 16),
    )
    dq, dk, dv, gq, gk = pl.pallas_call(
        hand_over,
        out_shape=(big, big, big, row, row),
        in_specs=[vmem] * 5,
        out_specs=(pl.BlockSpec(memory_space=pltpu.HBM),) * 5,
        scratch_shapes=[dma((5,))],
        compiler_params=pltpu.CompilerParams(vmem_limit_bytes=60 * 2**20),
    )(*[pltpu.with_memory_space_constraint(r, pltpu.VMEM) for r in results])
    return dq, dk, dv, gq.reshape(D), gk.reshape(D)


def solution(mesh):
    tokens = P("dp", "seq", None)
    return jax.shard_map(
        per_device,
        mesh=mesh,
        in_specs=(
            tokens, tokens, tokens, P(), P(), tokens, tokens, tokens, P("dp"), P(), P(),
        ),
        out_specs=(tokens, tokens, tokens, P(), P()),
        check_vma=False,
    )
```

```python
import functools
import math

import jax
import jax.numpy as jnp
from jax import lax
from jax.experimental import pallas as pl
from jax.experimental.pallas import tpu as pltpu
from jax.sharding import PartitionSpec as P

MESH = pl.DeviceIdType.MESH
F32 = jnp.float32
BF16 = jnp.bfloat16
STEPS = 10
EPS = 1e-6
NY, NZ = 2, 8
DZ = (4, 5, 3, 6, 2, 7, 1, 0)
BACK = (0, 2, 1, 4, 3, 6, 5, 7)
TOK, D = 128, 128
ROWS = 2048
CHUNKS = 2
TC = TOK // CHUNKS
RC = ROWS // CHUNKS
TILE = 256
GROUPS = RC // 128
SCALE = 1.0 / math.sqrt(D)
LOG2E = math.log2(math.e)
LEAD = 1

KINDS = ("k", "q", "v", "u0", "u1", "w0", "w1", "dq0", "dq1", "dv", "dk", "gs", "gd", "gt")
ROW = {name: i for i, name in enumerate(KINDS)}


def ring_step(t):
    odd = lax.rem(t, 2)
    half = NZ // 2
    return lax.rem(odd * (half + (t + 1) // 2) + (1 - odd) * (half - t // 2), NZ)


def dot(a, b, dims):
    return lax.dot_general(a, b, (dims, ((), ())), preferred_element_type=F32)


def kernel(
    q_in, k_in, v_in, noise_in, codes_in, exps_in, qg_ref, kg_ref, step_ref, rew_ref, gid_ref,
    dq_out, dk_out, dv_out, gq_out, gk_out,
    k_buf, v_buf, q_buf, u_buf, u_src, noise_v, codes_v, exps_v,
    kn, qn, qn_t, attn, d_t, g_nat, g_t, probs, probs_b, ds, dq_buf, dk_buf, dv_buf,
    nsq, part, parts, weights, gain_src, gains, gain_clip, gains2, gain_all,
    load_sem, send_sem, recv_sem,
):
    me = lax.axis_index("seq")
    clip = lax.axis_index("dp")
    y, z = me // NZ, lax.rem(me, NZ)
    home = 2 * (NZ - 1) + y

    def at(m, yy):
        return yy * NZ + lax.rem(z + DZ[m], NZ)

    def others():
        for m in range(NZ - 1):
            for yy in range(NY):
                yield at(m, yy), 2 * BACK[m] + y
        yield (1 - y) * NZ + z, home

    def remote(kind, src, dst, peer, axis="seq"):
        return pltpu.make_async_remote_copy(
            src_ref=src, dst_ref=dst, send_sem=send_sem.at[ROW[kind]], recv_sem=recv_sem.at[ROW[kind]],
            device_id={axis: peer}, device_id_type=MESH,
        )

    def send(kind, src, dst, peer, axis="seq"):
        remote(kind, src, dst, peer, axis).start()

    def own(kind, src, dst):
        pltpu.make_async_copy(src, dst, recv_sem.at[ROW[kind]]).start()

    def await_all(kind, ref):
        remote(kind, ref, ref, me).wait_recv()

    def await_sent(kind, ref):
        remote(kind, ref, ref, me).wait_send()

    loads = [
        pltpu.make_async_copy(noise_in.at[0], noise_v, load_sem.at[0]),
        pltpu.make_async_copy(codes_in.at[0], codes_v, load_sem.at[1]),
        pltpu.make_async_copy(exps_in.at[0], exps_v, load_sem.at[2]),
    ]
    for c in loads:
        c.start()

    barrier = pltpu.get_barrier_semaphore()
    for peer, _ in others():
        pl.semaphore_signal(barrier, inc=1, device_id={"seq": peer}, device_id_type=MESH)

    @pl.when(me == LEAD)
    def _():
        for j in range(1, 16):
            pl.semaphore_signal(
                barrier, inc=1, device_id={"dp": lax.rem(clip + j, 16)}, device_id_type=MESH
            )
        pl.semaphore_wait(barrier, 30)

    @pl.when(me != LEAD)
    def _():
        pl.semaphore_wait(barrier, 15)

    def cols(ref, head):
        return ref.at[0, :, pl.ds(pl.multiple_of(head * D, D), D)]

    def halves_of(ref, head):
        return ref.at[:, :, pl.ds(pl.multiple_of(head * D, D), D)]

    for peer, there in others():
        send("k", cols(k_in, peer), k_buf.at[there], peer)
    own("k", cols(k_in, me), k_buf.at[home])
    for peer, there in others():
        send("q", halves_of(q_in, peer), q_buf.at[:, there], peer)
    own("q", halves_of(q_in, me), q_buf.at[:, home])
    for peer, there in others():
        send("v", cols(v_in, peer), v_buf.at[there], peer)
    own("v", cols(v_in, me), v_buf.at[home])

    level = 1.0 - jnp.broadcast_to(step_ref[...].astype(F32), (1, 128)) / STEPS
    step_size = 1.0 / STEPS
    ratio = step_size / (0.7 * jnp.sqrt(step_size * level / (1.0 - level)))
    gid = gid_ref[...].astype(F32)
    rewards = rew_ref[...]
    picked = (lax.broadcasted_iota(jnp.int32, gid.shape, 1) == clip).astype(F32)
    own_gid = jnp.sum(picked * gid, axis=1, keepdims=True)
    same = (gid == own_gid).astype(F32)
    advantage = jnp.sum(picked * rewards, axis=1, keepdims=True) - jnp.sum(
        same * rewards, axis=1, keepdims=True
    ) / jnp.sum(same, axis=1, keepdims=True)

    for c in loads:
        c.wait()
    scales = jnp.transpose(jnp.exp2(exps_v[...].astype(F32)))
    noise_sq = jnp.zeros((TOK, D), F32)
    for h in range(16):
        code = codes_v[:, h * D:(h + 1) * D]
        magnitude = ((8 + (code & 7)) << ((code >> 3) & 15)).astype(F32) * (1.0 / 1024.0)
        old = jnp.where(code >= 128, -magnitude, magnitude) * scales[:, h:h + 1]
        noise = noise_v[:, h * D:(h + 1) * D].astype(F32)
        u_src[h] = (noise - ratio * old.astype(BF16).astype(F32)).astype(BF16)
        noise_sq = noise_sq + noise * noise
    nsq[...] = jnp.sum(jnp.transpose(noise_sq), axis=0, keepdims=True)

    def send_u(c, targets):
        rows = pl.ds(c * TC, TC)
        for peer, there in targets:
            send("u%d" % c, u_src.at[peer, rows], u_buf.at[c, there], peer)

    targets = list(others())
    early, late = targets[:10], targets[10:]
    send_u(0, targets)
    send_u(1, early)
    for c in range(CHUNKS):
        own("u%d" % c, u_src.at[me, pl.ds(c * TC, TC)], u_buf.at[c, home])

    def normed(x, gain):
        rinv = lax.rsqrt(jnp.mean(x * x, axis=1, keepdims=True) + EPS)
        return (gain * x * rinv).astype(BF16)

    await_all("k", k_buf)

    @pl.loop(0, 16, unroll=4)
    def _(n):
        kn[pl.ds(pl.multiple_of(n * D, D), D), :] = normed(k_buf[n].astype(F32), kg_ref[...])

    await_all("q", q_buf)

    def block(ref, g):
        c, m = g // GROUPS, lax.rem(g, GROUPS)
        return ref[c, pl.ds(m * CHUNKS, CHUNKS)].reshape(128, D)

    def rows_of(g, size=128):
        return pl.ds(pl.multiple_of(g * size, size), size)

    @pl.loop(0, 16, unroll=4)
    def _(g):
        x = normed(block(q_buf, g).astype(F32), qg_ref[...])
        qn[rows_of(g), :] = x
        qn_t[:, rows_of(g)] = jnp.transpose(x.astype(F32)).astype(BF16)

    @pl.loop(0, ROWS // TILE)
    def _(i):
        rows = rows_of(i, TILE)
        s = dot(qn[rows, :], kn[...], ((1,), (1,)))
        e = jnp.exp2((s - jnp.max(s, axis=1, keepdims=True)) * (SCALE * LOG2E))
        p = e * (1.0 / jnp.sum(e, axis=1, keepdims=True))
        probs[rows, :] = p
        probs_b[rows, :] = p.astype(BF16)

    await_all("v", v_buf)

    def values():
        return v_buf[...].reshape(ROWS, D)

    @pl.loop(0, ROWS // TILE)
    def _(i):
        rows = rows_of(i, TILE)
        attn[rows, :] = dot(probs_b[rows, :], values(), ((1,), (0,))).astype(BF16)

    for c in range(CHUNKS):
        await_all("u%d" % c, u_buf.at[c])

        @pl.loop(0, GROUPS, unroll=4)
        def _(m, c=c):
            g = c * GROUPS + m
            rows = rows_of(g)
            x = block(u_buf, g).astype(F32) + ratio * attn[rows, :].astype(F32)
            x_t = jnp.transpose(x)
            d_t[:, rows] = x_t
            part[c, pl.ds(lax.rem(z + ring_step(m), NZ), 1), :] = jnp.sum(
                x_t * x_t, axis=0, keepdims=True
            )

        line = nsq[...]
        halves = jnp.where(y == c, line, jnp.concatenate([line[:, TC:], line[:, :TC]], axis=1))
        shape = (GROUPS, 128)
        here = (lax.broadcasted_iota(jnp.int32, shape, 0) == z) & (
            lax.broadcasted_iota(jnp.int32, shape, 1) // TC == y
        )
        mine = part[c] - jnp.where(here, jnp.broadcast_to(halves, shape), 0.0)
        part[c] = mine
        parts[c, me] = mine
        for peer, _ in others():
            send("w%d" % c, part.at[c], parts.at[c, me], peer)
        if c == 0:
            send_u(1, late)

    def weigh(c):
        await_all("w%d" % c, parts.at[c, pl.ds(0, 15)])
        total = jnp.sum(parts[c], axis=0)
        weights[c] = advantage * jnp.exp(total * (-1.0 / (2.0 * ROWS))) * ratio

    def weigh_block(g):
        c, m = g // GROUPS, lax.rem(g, GROUPS)
        rows = rows_of(g)
        w = weights[c, pl.ds(lax.rem(z + ring_step(m), NZ), 1), :]
        x = w * d_t[:, rows]
        g_t[:, rows] = x.astype(BF16)
        g_nat[rows, :] = jnp.transpose(x).astype(BF16)

    def out_copy(kind, src, dst, peer):
        @pl.when(peer != me)
        def _():
            send(kind, src, dst, peer)

        @pl.when(peer == me)
        def _():
            own(kind, src, dst)

    def own_cols(ref):
        return ref.at[0, :, pl.ds(pl.multiple_of(me * D, D), D)]

    def own_piece(ref, c):
        return ref.at[0, pl.ds(c * TC, TC), pl.ds(pl.multiple_of(me * D, D), D)]

    def norm_back(x, gain, grad):
        rinv = lax.rsqrt(jnp.mean(x * x, axis=1, keepdims=True) + EPS)
        scaled = gain * grad
        inner = jnp.sum(scaled * x, axis=1, keepdims=True)
        out = rinv * scaled - x * (rinv * rinv * rinv * inner * (1.0 / D))
        return out.astype(BF16), jnp.sum(grad * x * rinv, axis=0, keepdims=True)

    def dscore_rows(i):
        rows = rows_of(i, TILE)
        g = g_nat[rows, :]
        delta = jnp.sum(g.astype(F32) * attn[rows, :].astype(F32), axis=1, keepdims=True)
        dp = dot(g, values(), ((1,), (1,)))
        ds[rows, :] = (probs[rows, :] * (dp - delta)).astype(BF16)

    per_tile = TILE // TC

    def query_rows(c, i):
        rows = rows_of(c * (RC // TILE) + i, TILE)
        grad = dot(ds[rows, :], kn[...], ((1,), (0,))) * SCALE
        x = q_buf[c, pl.ds(i * per_tile, per_tile)].reshape(TILE, D).astype(F32)
        out, gain = norm_back(x, qg_ref[...], grad)
        dq_buf[c, pl.ds(i * per_tile, per_tile)] = out.reshape(per_tile, TC, D)
        gain_src[0:1, :] = gain_src[0:1, :] + gain

    def send_query_rows(c, i):
        for j in range(per_tile):
            slot = i * per_tile + j
            peer = (j % NY) * NZ + lax.rem(z + ring_step(slot // 2), NZ)
            out_copy("dq%d" % c, dq_buf.at[c, slot], own_piece(dq_out, c), peer)

    gain_src[...] = jnp.zeros_like(gain_src)

    weigh(0)

    @pl.loop(0, RC // TILE)
    def _(i):
        for j in range(TILE // 128):
            weigh_block(i * (TILE // 128) + j)
        dscore_rows(i)
        query_rows(0, i)
        send_query_rows(0, i)

    weigh(1)

    @pl.loop(GROUPS, 2 * GROUPS, unroll=4)
    def _(g):
        weigh_block(g)

    @pl.loop(0, NZ)
    def _(t):
        wide = rows_of(t, 256)
        acc = dot(g_t[...], probs_b[:, wide], ((1,), (0,)))
        for j in range(NY):
            slot = t * NY + j
            dv_buf[slot] = jnp.transpose(acc[:, j * D:(j + 1) * D]).astype(BF16)
            peer = j * NZ + lax.rem(z + ring_step(t), NZ)
            out_copy("dv", dv_buf.at[slot], own_cols(dv_out), peer)

    @pl.loop(0, RC // TILE)
    def _(i):
        dscore_rows(RC // TILE + i)
        query_rows(1, i)

    @pl.loop(0, NZ)
    def _(t):
        wide = rows_of(t, 256)
        acc = dot(qn_t[...], ds[:, wide], ((1,), (0,)))
        for j in range(NY):
            slot = t * NY + j
            grad = jnp.transpose(acc[:, j * D:(j + 1) * D]) * SCALE
            out, gain = norm_back(k_buf[slot].astype(F32), kg_ref[...], grad)
            dk_buf[slot] = out
            gain_src[1:2, :] = gain_src[1:2, :] + gain

    @pl.when(me != LEAD)
    def _():
        send("gs", gain_src, gains.at[me], LEAD)

    @pl.when(me == LEAD)
    def _():
        gains[me] = gain_src[...]

    def send_keys(first, last):
        @pl.loop(first, last)
        def _(t):
            for j in range(NY):
                slot = t * NY + j
                peer = j * NZ + lax.rem(z + ring_step(t), NZ)
                out_copy("dk", dk_buf.at[slot], own_cols(dk_out), peer)

    send_keys(0, NZ // 2)

    @pl.when(me == LEAD)
    def _():
        await_all("gs", gains.at[pl.ds(0, 15)])
        total = jnp.sum(gains[...], axis=0)
        gain_clip[...] = total
        gains2[clip] = total
        for j in range(1, 16):
            send("gd", gain_clip, gains2.at[clip], lax.rem(clip + j, 16), "dp")

    send_keys(NZ // 2, NZ)

    @pl.loop(0, RC // TILE - 1)
    def _(i):
        send_query_rows(1, i)

    @pl.when(me == LEAD)
    def _():
        await_all("gd", gains2.at[pl.ds(0, 15)])
        gain_all[...] = jnp.sum(gains2[...], axis=0) * (1.0 / math.sqrt(16.0 * 16.0 * ROWS))
        for peer, _ in others():
            send("gt", gain_all, gain_all, peer)

    send_query_rows(1, RC // TILE - 1)

    for kind, ref in (
        ("k", k_buf.at[pl.ds(0, 15)]), ("q", q_buf.at[:, pl.ds(0, 15)]), ("v", v_buf.at[pl.ds(0, 15)]),
        ("u0", u_buf.at[0, pl.ds(0, 15)]), ("u1", u_buf.at[1, pl.ds(0, 15)]),
        ("w0", parts.at[0, pl.ds(0, 15)]), ("w1", parts.at[1, pl.ds(0, 15)]),
    ):
        await_sent(kind, ref)

    @pl.when(me == LEAD)
    def _():
        await_sent("gd", gains2.at[pl.ds(0, 15)])
        await_sent("gt", gains2.at[pl.ds(0, 15)])

    @pl.when(me != LEAD)
    def _():
        await_sent("gs", gain_src)
        await_all("gt", gain_all)

    gq_out[...] = gain_all[0:1, :]
    gk_out[...] = gain_all[1:2, :]

    for kind, buf, out in (
        ("dv", dv_buf.at[pl.ds(0, 15)], dv_out), ("dk", dk_buf.at[pl.ds(0, 15)], dk_out),
        ("dq0", dq_buf.at[0, pl.ds(0, 15)], dq_out.at[0, pl.ds(0, TC)]),
        ("dq1", dq_buf.at[1, pl.ds(0, 15)], dq_out.at[0, pl.ds(TC, TC)]),
    ):
        await_all(kind, out)
        await_sent(kind, buf)


def hand_over(*refs):
    n = (len(refs) - 1) // 2
    copies = [pltpu.make_async_copy(refs[i], refs[n + i], refs[-1].at[i]) for i in range(n)]
    for c in copies:
        c.start()
    for c in copies:
        c.wait()


def per_device(q, k, v, q_gain, k_gain, noise, codes, exps, step, rewards, gids):
    hbm, vmem = pl.BlockSpec(memory_space=pl.ANY), pl.BlockSpec(memory_space=pltpu.VMEM)
    big = jax.ShapeDtypeStruct((1, TOK, 16 * D), BF16)
    row = jax.ShapeDtypeStruct((1, D), F32)
    dma = pltpu.SemaphoreType.DMA
    halves = (CHUNKS, 16, TC, D)
    results = pl.pallas_call(
        kernel,
        out_shape=(pltpu.VMEM((1, TOK, 16 * D), BF16),) * 3 + (pltpu.VMEM((1, D), F32),) * 2,
        in_specs=[pl.BlockSpec(memory_space=pltpu.HBM)] * 6 + [vmem] * 5,
        out_specs=(vmem,) * 5,
        scratch_shapes=[
            pltpu.VMEM((16, TOK, D), BF16),
            pltpu.VMEM((16, TOK, D), BF16),
            pltpu.VMEM(halves, BF16),
            pltpu.VMEM(halves, BF16),
            pltpu.VMEM((16, TOK, D), BF16),
            pltpu.VMEM((TOK, 16 * D), BF16),
            pltpu.VMEM((TOK, 16 * D), jnp.int32),
            pltpu.VMEM((16, TOK), jnp.int32),
            pltpu.VMEM((ROWS, D), BF16),
            pltpu.VMEM((ROWS, D), BF16),
            pltpu.VMEM((D, ROWS), BF16),
            pltpu.VMEM((ROWS, D), BF16),
            pltpu.VMEM((D, ROWS), F32),
            pltpu.VMEM((ROWS, D), BF16),
            pltpu.VMEM((D, ROWS), BF16),
            pltpu.VMEM((ROWS, ROWS), F32),
            pltpu.VMEM((ROWS, ROWS), BF16),
            pltpu.VMEM((ROWS, ROWS), BF16),
            pltpu.VMEM(halves, BF16),
            pltpu.VMEM((16, TOK, D), BF16),
            pltpu.VMEM((16, TOK, D), BF16),
            pltpu.VMEM((1, 128), F32),
            pltpu.VMEM((CHUNKS, GROUPS, 128), F32),
            pltpu.VMEM((CHUNKS, 16, GROUPS, 128), F32),
            pltpu.VMEM((CHUNKS, GROUPS, 128), F32),
            pltpu.VMEM((8, 128), F32),
            pltpu.VMEM((16, 8, 128), F32),
            pltpu.VMEM((8, 128), F32),
            pltpu.VMEM((16, 8, 128), F32),
            pltpu.VMEM((8, 128), F32),
            dma((3,)),
            dma((len(KINDS),)),
            dma((len(KINDS),)),
        ],
        compiler_params=pltpu.CompilerParams(
            collective_id=0, has_side_effects=True, vmem_limit_bytes=56 * 2**20
        ),
    )(
        q.reshape(CHUNKS, TC, 16 * D), k, v, noise, codes, jnp.swapaxes(exps, 1, 2), q_gain.reshape(1, D), k_gain.reshape(1, D),
        step.reshape(1, 1), rewards.reshape(1, 16), gids.reshape(1, 16),
    )
    dq, dk, dv, gq, gk = pl.pallas_call(
        hand_over,
        out_shape=(big, big, big, row, row),
        in_specs=[vmem] * 5,
        out_specs=(pl.BlockSpec(memory_space=pltpu.HBM),) * 5,
        scratch_shapes=[dma((5,))],
        compiler_params=pltpu.CompilerParams(vmem_limit_bytes=60 * 2**20),
    )(*[pltpu.with_memory_space_constraint(r, pltpu.VMEM) for r in results])
    return dq, dk, dv, gq.reshape(D), gk.reshape(D)


def solution(mesh):
    tokens = P("dp", "seq", None)
    return jax.shard_map(
        per_device,
        mesh=mesh,
        in_specs=(
            tokens, tokens, tokens, P(), P(), tokens, tokens, tokens, P("dp"), P(), P(),
        ),
        out_specs=(tokens, tokens, tokens, P(), P()),
        check_vma=False,
    )
```
